256 devices in a mesh: dp: 64 (over z, x, core), ctx: 4 (over y).
Axes of the slice: x: 4, y: 4, z: 8, core: 2. Of those that a mesh axis runs over, the one named last changes fastest.
Arguments:
- projected: bfloat16 [32768, 6144], P(('dp', 'ctx')), may hold values from -16 to 16
- out_grad: bfloat16 [32768, 2048], P(('dp', 'ctx')), may hold values from -6 to 6
- dest_row: int32 [32768], P(('dp', 'ctx')), may hold values from 0 to 32767, as said below
- lengths: int32 [64, 3], P('dp'), may hold values from 1 to 384, 512 in all within a row
Outputs:
- attended: bfloat16 [32768, 2048], P(('dp', 'ctx'))
- grad_projected: bfloat16 [32768, 6144], P(('dp', 'ctx'))
The draws below stay inside these ranges and needn't reach their ends.
Inputs may be any that keep to these rules, and one draw needn't show every extreme that they name: Rollout rows move to dealt rows in aligned runs of 1; dest_row is a permutation of all rows; a row keeps its place along ctx: (dest_row[i] // 128) % 4 equals (i // 128) % 4; of the 128 rows of one device at most 3 go to one scorer group, and every device sends exactly 3 rows to some group.
All inputs are finite; a program needn't handle non-finite values.
Results may differ from the reference program's by a relative error of at most 0.007.
Values may be sent and summed in bfloat16 or wider, within the bound.
No kernel may reach another device: no remote copies, remote signals or barrier semaphores. Data moves between devices by JAX's collectives and lax.ppermute only.
A program may use at most 64 MiB of HBM per device.

```python
import math
import jax
import jax.numpy as jnp
import numpy as np
from jax import lax

HEADS = 16
HDIM = 128
TOK_DEV = 128
UNIT = 1
COMPS = 3
GROUPS = 64
SPLIT = 4
GROUP_ROWS = 512
TOKENS = 32768


def draw_dest_row(key, part):
    key = jax.random.fold_in(key, 11)
    units = TOK_DEV // UNIT
    average = units // GROUPS
    quarter = GROUPS // 4

    def column_plan(column_key):
        first_key, second_key, third_key = jax.random.split(column_key, 3)
        order = jax.random.permutation(first_key, GROUPS)
        ranked = jnp.arange(GROUPS)
        counts = jnp.where(ranked < quarter, average + average // 2, jnp.where(ranked < 2 * quarter, average - average // 2, average))
        listed = jnp.repeat(order, counts, total_repeat_length=units)
        shifts = jax.random.permutation(second_key, listed)
        placings = jax.vmap(lambda inner_key: jax.random.permutation(inner_key, units))(jax.random.split(third_key, GROUPS))
        return (shifts, placings)
    shifts, placings = jax.vmap(column_plan)(jax.random.split(key, SPLIT))
    source = jnp.arange(GROUPS)[:, None, None]
    column = jnp.arange(SPLIT)[None, :, None]
    within = jnp.arange(units)[None, None, :]
    target = (source + shifts[None, :, :]) % GROUPS
    placing = placings[column, target, within]
    starts = ((target * SPLIT + column) * units + placing) * UNIT
    rows_all = starts[..., None] + jnp.arange(UNIT)
    return rows_all.reshape(TOKENS).astype(jnp.int32)


def draw_projected(key, part):
    key = jax.random.fold_in(key, 23)
    width = HEADS * HDIM
    base_key = jax.random.fold_in(key, 0)
    factors = jnp.array([1.0, 2.0, 1.0], jnp.float32)[None, :, None]
    base = jnp.clip(jax.random.normal(base_key, (TOKENS, 3, width), jnp.float32), -4.0, 4.0) * factors
    return base.reshape(TOKENS, 3 * width).astype(jnp.bfloat16)


def block_scale(rng, extent, shards, low, top_value):
    loudness, own = 1.0, jax.random.fold_in(rng, 6)
    for axis_at, parts in shards:
        heights = jnp.exp(jax.random.uniform(jax.random.fold_in(own, axis_at), (parts,), jnp.float32, low / len(shards), top_value / len(shards)))
        loudness = loudness * jnp.repeat(heights, extent[axis_at] // parts).reshape([-1 if axis == axis_at else 1 for axis in range(len(extent))])
    return loudness


def profile(number_of, total, reach, skew):
    loads = [(1 << 20) // math.isqrt(rank ** skew) + 1 for rank in range(2, number_of + 1)]
    surplus, given = total - reach - (number_of - 1), [1] * (number_of - 1)
    while surplus > 0:
        free = [i for i in range(number_of - 1) if given[i] < reach]
        whole, left = sum([loads[i] for i in free]), surplus
        for i in free:
            addition = min(reach - given[i], max(1, left * loads[i] // whole), surplus)
            given[i] = given[i] + addition
            surplus = surplus - addition
    return np.array([reach] + given)


def ragged(rng, amount, total, bound, slope):
    if amount == 2:
        one = jax.random.randint(rng, (), max(1, total - bound), min(bound, total - 1) + 1)
        return jnp.stack([one, total - one])
    tallies = jnp.asarray(profile(amount, total, bound, slope), jnp.int32)
    couples = (amount - 1) // 2
    giver, receiver = tallies[1:1 + 2 * couples:2], tallies[2:2 + 2 * couples:2]
    slack = jnp.minimum(giver - 1, bound - receiver)
    passed = jax.random.randint(jax.random.fold_in(rng, 1), (couples,), 0, 1 << 20) % (slack + 1)
    tallies = tallies.at[1:1 + 2 * couples:2].set(giver - passed).at[2:2 + 2 * couples:2].set(receiver + passed)
    return tallies[jax.random.permutation(jax.random.fold_in(rng, 2), amount)]


def centred(key, extent, deviation, most, shards=(), kind=jnp.bfloat16):
    entries = deviation * jax.random.normal(key, extent, jnp.float32)
    if shards:
        entries = entries * block_scale(key, extent, shards, -0.22, 0.18)
    return jnp.clip(entries, -most, most).astype(kind)


def setup_inputs(seed: int = 0) -> dict:
    key_of = jax.random.split(jax.random.key(seed), 5)
    projected = draw_projected(jax.random.fold_in(key_of[4], 71), 0)
    out_grad = centred(key_of[1], (TOKENS, HEADS * HDIM), 1.0, 6.0, ((0, 256),))
    dest_row = draw_dest_row(jax.random.fold_in(key_of[4], 71), 0)
    lengths = jax.vmap(lambda own: ragged(own, COMPS, GROUP_ROWS, GROUP_ROWS - 128, 2))(jax.random.split(key_of[3], GROUPS)).reshape((GROUPS, COMPS)).astype(jnp.int32)
    return dict(projected=projected, out_grad=out_grad, dest_row=dest_row, lengths=lengths)


lowest = -1e+30

def rounded(values):
    return lax.optimization_barrier(values.astype(jnp.bfloat16)).astype(jnp.float32)

def attend_group(entry):
    proj_rows, cotangent_rows, spans = entry
    width = HEADS * HDIM
    scale = 1.0 / math.sqrt(HDIM)
    queries = proj_rows[:, :width].reshape(GROUP_ROWS, HEADS, HDIM).astype(jnp.float32)
    keys = proj_rows[:, width:2 * width].reshape(GROUP_ROWS, HEADS, HDIM).astype(jnp.float32)
    values = proj_rows[:, 2 * width:].reshape(GROUP_ROWS, HEADS, HDIM).astype(jnp.float32)
    cotangent = cotangent_rows.reshape(GROUP_ROWS, HEADS, HDIM).astype(jnp.float32)
    ends = jnp.cumsum(spans)
    positions = jnp.arange(GROUP_ROWS, dtype=jnp.int32)
    segment = lax.optimization_barrier(jnp.sum((positions[:, None] >= ends[None, :]).astype(jnp.int32), axis=1))
    allowed = (segment[:, None] == segment[None, :])[None]
    scores = jnp.einsum('qhd,khd->hqk', queries, keys) * scale
    masked = jnp.where(allowed, scores, lowest)
    top = lax.optimization_barrier(jnp.max(masked, axis=2, keepdims=True))
    log_total = top + jnp.log(lax.optimization_barrier(jnp.sum(jnp.where(allowed, jnp.exp(masked - top), 0.0), axis=2, keepdims=True)))
    exact_weights = jnp.where(allowed, jnp.exp(scores - log_total), 0.0)
    weights = rounded(exact_weights)
    mixed = jnp.einsum('hqk,khd->qhd', weights, values)
    drift = lax.optimization_barrier(jnp.sum(cotangent * mixed, axis=2))
    pulls = jnp.einsum('qhd,khd->hqk', cotangent, values)
    slopes = rounded(exact_weights * (pulls - jnp.transpose(drift)[:, :, None]) * scale)
    query_grad = jnp.einsum('hqk,khd->qhd', slopes, keys)
    blocks = GROUP_ROWS // TOK_DEV
    key_partial = rounded(jnp.einsum('hsqk,sqhd->skhd', slopes.reshape(HEADS, blocks, TOK_DEV, GROUP_ROWS), queries.reshape(blocks, TOK_DEV, HEADS, HDIM)))
    value_partial = rounded(jnp.einsum('hsqk,sqhd->skhd', weights.reshape(HEADS, blocks, TOK_DEV, GROUP_ROWS), cotangent.reshape(blocks, TOK_DEV, HEADS, HDIM)))
    key_grad = lax.optimization_barrier(jnp.sum(key_partial, axis=0))
    value_grad = lax.optimization_barrier(jnp.sum(value_partial, axis=0))
    output_rows = mixed.reshape(GROUP_ROWS, width).astype(jnp.bfloat16)
    grad_rows = jnp.concatenate([query_grad.reshape(GROUP_ROWS, width), key_grad.reshape(GROUP_ROWS, width), value_grad.reshape(GROUP_ROWS, width)], axis=1).astype(jnp.bfloat16)
    return (output_rows, grad_rows)

def reference(projected, out_grad, dest_row, lengths):
    width = HEADS * HDIM
    dealt_projected = jnp.zeros_like(projected).at[dest_row].set(projected)
    dealt_cotangent = jnp.zeros_like(out_grad).at[dest_row].set(out_grad)
    outputs, gradients = lax.map(attend_group, (dealt_projected.reshape(GROUPS, GROUP_ROWS, 3 * width), dealt_cotangent.reshape(GROUPS, GROUP_ROWS, width), lengths))
    attended = outputs.reshape(TOKENS, width)[dest_row]
    grad_projected = gradients.reshape(TOKENS, 3 * width)[dest_row]
    return (attended, grad_projected)
```

```python
import math

import jax
import jax.numpy as jnp
from jax import lax
from jax.experimental import pallas as pl
from jax.experimental.pallas import tpu as pltpu
from jax.sharding import PartitionSpec as P

HEADS = 16
HDIM = 128
SLOTS = 3
LOWEST = -1e30
VMEM_LIMIT = 56 * 1024 * 1024


def swap_matrix(side):
    rows = lax.broadcasted_iota(jnp.int32, (side * side, side * side), 0)
    cols = lax.broadcasted_iota(jnp.int32, (side * side, side * side), 1)
    partner = (rows % side) * side + rows // side
    return (cols == partner).astype(jnp.bfloat16)


def matmul(left, right):
    return jnp.dot(left, right, preferred_element_type=jnp.float32)


def matmul_nt(left, right):
    return lax.dot_general(
        left, right, (((1,), (1,)), ((), ())), preferred_element_type=jnp.float32
    )


def slot_of_rows(dest, groups, contexts, rows):
    target = dest // (rows * contexts)
    across = jnp.broadcast_to(target.astype(jnp.float32), (rows, rows))
    down = jnp.transpose(across)
    earlier = lax.broadcasted_iota(jnp.int32, (rows, rows), 0) < lax.broadcasted_iota(
        jnp.int32, (rows, rows), 1
    )
    same = jnp.where(jnp.logical_and(across == down, earlier), 1.0, 0.0)
    rank = jnp.sum(same, axis=0, keepdims=True).astype(jnp.int32)
    return rank * groups + target


def pack_kernel(groups, contexts, proj_ref, cot_ref, dest_ref, out_ref):
    rows = proj_ref.shape[0]
    width = cot_ref.shape[1]
    part = width // contexts
    pieces = 4 * part // HDIM
    slot = slot_of_rows(dest_ref[...], groups, contexts, rows)
    slots = SLOTS * groups
    pick = (lax.broadcasted_iota(jnp.int32, (slots, rows), 0) == slot).astype(jnp.bfloat16)
    swap = swap_matrix(pieces)
    for share in range(contexts):
        begin = share * part
        picked = [
            matmul(pick, block).astype(jnp.bfloat16)
            for block in (
                proj_ref[:, begin : begin + part],
                proj_ref[:, width + begin : width + begin + part],
                proj_ref[:, 2 * width + begin : 2 * width + begin + part],
                cot_ref[:, begin : begin + part],
            )
        ]
        picked = jnp.concatenate(picked, axis=1)
        for rank in range(SLOTS):
            chunks = []
            for first in range(rank * groups, (rank + 1) * groups, pieces):
                chunks.append(
                    jnp.concatenate(
                        [
                            picked[first : first + pieces, j * HDIM : (j + 1) * HDIM]
                            for j in range(pieces)
                        ],
                        axis=0,
                    )
                )
            swapped = matmul(swap, jnp.concatenate(chunks, axis=1)).astype(jnp.bfloat16)
            for at in range(groups // pieces):
                out_ref[
                    at * pieces : (at + 1) * pieces, share, rank * pieces : (rank + 1) * pieces, :
                ] = swapped[:, at * HDIM : (at + 1) * HDIM].reshape(pieces, pieces, HDIM)


def unpack_kernel(groups, contexts, in_ref, dest_ref, attended_ref, grad_ref):
    rows, width = attended_ref.shape
    part = width // contexts
    pieces = 4 * part // HDIM
    slot = slot_of_rows(dest_ref[...], groups, contexts, rows)
    slots = SLOTS * groups
    slot_down = jnp.transpose(jnp.broadcast_to(slot.astype(jnp.float32), (rows, rows)))[:, :1]
    pick = (
        lax.broadcasted_iota(jnp.int32, (rows, slots), 1) == slot_down.astype(jnp.int32)
    ).astype(jnp.bfloat16)
    swap = swap_matrix(pieces)
    for share in range(contexts):
        stacked = []
        for rank in range(SLOTS):
            chunks = jnp.concatenate(
                [
                    in_ref[
                        first : first + pieces, share, rank * pieces : (rank + 1) * pieces, :
                    ].reshape(pieces * pieces, HDIM)
                    for first in range(0, groups, pieces)
                ],
                axis=1,
            )
            swapped = matmul(swap, chunks).astype(jnp.bfloat16)
            for at in range(groups // pieces):
                stacked.append(
                    jnp.concatenate(
                        [
                            swapped[j * pieces : (j + 1) * pieces, at * HDIM : (at + 1) * HDIM]
                            for j in range(pieces)
                        ],
                        axis=1,
                    )
                )
        result = matmul(pick, jnp.concatenate(stacked, axis=0)).astype(jnp.bfloat16)
        begin = share * part
        attended_ref[:, begin : begin + part] = result[:, :part]
        for t in range(3):
            grad_ref[:, t * width + begin : t * width + begin + part] = result[
                :, (t + 1) * part : (t + 2) * part
            ]


def attend_kernel(contexts, in_ref, dest_ref, lengths_ref, out_ref, slot_ref, back_ref):
    devices, local_rows = dest_ref.shape
    group_rows = local_rows * contexts
    pieces = in_ref.shape[1] // SLOTS
    heads = pieces // 4
    slots = SLOTS * devices
    group = lax.axis_index("dp")
    swap = swap_matrix(pieces)

    dest = dest_ref[...]
    mine = dest // group_rows == group
    place = (dest % group_rows).astype(jnp.float32)
    upto = (
        lax.broadcasted_iota(jnp.int32, (local_rows, local_rows), 0)
        <= lax.broadcasted_iota(jnp.int32, (local_rows, local_rows), 1)
    ).astype(jnp.bfloat16)
    counted = matmul(jnp.where(mine, 1.0, 0.0).astype(jnp.bfloat16), upto)
    downs, acrosses = [], []
    for rank in range(SLOTS):
        chosen = jnp.logical_and(mine, counted == rank + 1.0)
        down = jnp.sum(jnp.where(chosen, place + 1.0, 0.0), axis=1, keepdims=True) - 1.0
        downs.append(down)
        acrosses.append(jnp.transpose(jnp.broadcast_to(down, (devices, 128)))[:1, :])
    place_down = jnp.concatenate(downs, axis=0).astype(jnp.int32)
    place_across = jnp.concatenate(acrosses, axis=1).astype(jnp.int32)
    gather = (
        lax.broadcasted_iota(jnp.int32, (group_rows, slots), 0) == place_across
    ).astype(jnp.bfloat16)
    scatter = (
        lax.broadcasted_iota(jnp.int32, (slots, group_rows), 1) == place_down
    ).astype(jnp.bfloat16)

    for rank in range(SLOTS):
        for first in range(0, devices, 4 * pieces):
            chunks = jnp.concatenate(
                [
                    in_ref[
                        first + at * pieces : first + (at + 1) * pieces,
                        rank * pieces : (rank + 1) * pieces,
                        :,
                    ].reshape(pieces * pieces, HDIM)
                    for at in range(4)
                ],
                axis=1,
            )
            swapped = matmul(swap, chunks).astype(jnp.bfloat16)
            for at in range(4):
                begin = rank * devices + first + at * pieces
                for j in range(pieces):
                    slot_ref[begin : begin + pieces, j * HDIM : (j + 1) * HDIM] = swapped[
                        j * pieces : (j + 1) * pieces, at * HDIM : (at + 1) * HDIM
                    ]

    end0 = lengths_ref[0, 0]
    end1 = end0 + lengths_ref[0, 1]
    end2 = end1 + lengths_ref[0, 2]

    def segment(shape, axis):
        position = lax.broadcasted_iota(jnp.int32, shape, axis)
        return (
            (position >= end0).astype(jnp.int32)
            + (position >= end1).astype(jnp.int32)
            + (position >= end2).astype(jnp.int32)
        )

    bias = jnp.where(
        segment((group_rows, group_rows), 0) == segment((group_rows, group_rows), 1), 0.0, LOWEST
    )
    scale = 1.0 / math.sqrt(HDIM)
    for head in range(heads):
        query, key, value, cotangent = [
            matmul(
                gather, slot_ref[:, (t * heads + head) * HDIM : (t * heads + head + 1) * HDIM]
            ).astype(jnp.bfloat16)
            for t in range(4)
        ]
        scores = matmul_nt(key, query) * (scale * math.log2(math.e)) + bias
        top = jnp.max(scores, axis=0, keepdims=True)
        powers = jnp.exp2(scores - top)
        total = jnp.sum(powers, axis=0, keepdims=True)
        exact = powers * (1.0 / total)
        weights = exact.astype(jnp.bfloat16)
        mixed = matmul(jnp.transpose(value), weights)
        drift = jnp.sum(
            jnp.transpose(cotangent).astype(jnp.float32) * mixed, axis=0, keepdims=True
        )
        pulls = matmul_nt(value, cotangent)
        slopes = (exact * ((pulls - drift) * scale)).astype(jnp.bfloat16)
        query_grad = matmul(jnp.transpose(key), slopes)
        key_grad = matmul(slopes, query)
        value_grad = matmul(weights, cotangent)
        results = (
            matmul_nt(scatter, mixed.astype(jnp.bfloat16)),
            matmul_nt(scatter, query_grad.astype(jnp.bfloat16)),
            matmul(scatter, key_grad.astype(jnp.bfloat16)),
            matmul(scatter, value_grad.astype(jnp.bfloat16)),
        )
        for t in range(4):
            j = t * heads + head
            back_ref[:, j * HDIM : (j + 1) * HDIM] = results[t].astype(jnp.bfloat16)

    for rank in range(SLOTS):
        for first in range(0, devices, 4 * pieces):
            chunks = []
            for at in range(4):
                begin = rank * devices + first + at * pieces
                chunks.append(
                    jnp.concatenate(
                        [
                            back_ref[begin : begin + pieces, j * HDIM : (j + 1) * HDIM]
                            for j in range(pieces)
                        ],
                        axis=0,
                    )
                )
            swapped = matmul(swap, jnp.concatenate(chunks, axis=1)).astype(jnp.bfloat16)
            for at in range(4):
                out_ref[
                    first + at * pieces : first + (at + 1) * pieces,
                    rank * pieces : (rank + 1) * pieces,
                    :,
                ] = swapped[:, at * HDIM : (at + 1) * HDIM].reshape(pieces, pieces, HDIM)


def on_device(projected, out_grad, dest_row, lengths):
    rows, width = out_grad.shape
    groups = lax.axis_size("dp")
    contexts = lax.axis_size("ctx")
    devices = groups * contexts
    part = width // contexts
    pieces = 4 * part // HDIM
    everyone = ("dp", "ctx")
    params = pltpu.CompilerParams(vmem_limit_bytes=VMEM_LIMIT)
    whole = pl.BlockSpec(memory_space=pltpu.VMEM)

    all_dest = lax.all_gather(dest_row, everyone, axis=0, tiled=True).reshape(devices, rows)
    dest = dest_row.reshape(1, rows)

    sent = pl.pallas_call(
        lambda *refs: pack_kernel(groups, contexts, *refs),
        out_shape=jax.ShapeDtypeStruct((groups, contexts, SLOTS * pieces, HDIM), jnp.bfloat16),
        in_specs=[whole] * 3,
        out_specs=whole,
        compiler_params=params,
        name="pack",
    )(projected, out_grad, dest)
    arrived = lax.all_to_all(
        sent.reshape(devices, SLOTS * pieces, HDIM), everyone, 0, 0, tiled=True
    )
    answers = pl.pallas_call(
        lambda *refs: attend_kernel(contexts, *refs),
        out_shape=jax.ShapeDtypeStruct((devices, SLOTS * pieces, HDIM), jnp.bfloat16),
        in_specs=[whole, whole, pl.BlockSpec(memory_space=pltpu.SMEM)],
        out_specs=whole,
        scratch_shapes=[
            pltpu.VMEM((SLOTS * devices, pieces * HDIM), jnp.bfloat16),
            pltpu.VMEM((SLOTS * devices, pieces * HDIM), jnp.bfloat16),
        ],
        compiler_params=params,
        name="attend",
    )(arrived, all_dest, lengths)
    returned = lax.all_to_all(answers, everyone, 0, 0, tiled=True)
    return pl.pallas_call(
        lambda *refs: unpack_kernel(groups, contexts, *refs),
        out_shape=(
            jax.ShapeDtypeStruct((rows, width), jnp.bfloat16),
            jax.ShapeDtypeStruct((rows, 3 * width), jnp.bfloat16),
        ),
        in_specs=[whole] * 2,
        out_specs=(whole, whole),
        compiler_params=params,
        name="unpack",
    )(returned.reshape(groups, contexts, SLOTS * pieces, HDIM), dest)


def solution(mesh):
    placed = (P(("dp", "ctx"), None), P(("dp", "ctx"), None), P(("dp", "ctx")), P("dp", None))
    return jax.shard_map(
        on_device,
        mesh=mesh,
        in_specs=placed,
        out_specs=(P(("dp", "ctx"), None), P(("dp", "ctx"), None)),
        check_vma=False,
    )
```

```python
import math

import jax
import jax.numpy as jnp
from jax import lax
from jax.experimental import pallas as pl
from jax.experimental.pallas import tpu as pltpu
from jax.sharding import PartitionSpec as P

HEADS = 16
HDIM = 128
SLOTS = 3
LOWEST = -1e30
VMEM_LIMIT = 56 * 1024 * 1024


def swap_matrix(side):
    rows = lax.broadcasted_iota(jnp.int32, (side * side, side * side), 0)
    cols = lax.broadcasted_iota(jnp.int32, (side * side, side * side), 1)
    partner = (rows % side) * side + rows // side
    return (cols == partner).astype(jnp.bfloat16)


def iota(shape, axis):
    return lax.broadcasted_iota(jnp.int32, shape, axis)


def matmul(left, right):
    return jnp.dot(left, right, preferred_element_type=jnp.float32)


def matmul_nt(left, right):
    return lax.dot_general(
        left, right, (((1,), (1,)), ((), ())), preferred_element_type=jnp.float32
    )


def slot_of_rows(dest, groups, contexts, rows):
    target = dest // (rows * contexts)
    across = jnp.broadcast_to(target.astype(jnp.float32), (rows, rows))
    down = jnp.transpose(across)
    earlier = lax.broadcasted_iota(jnp.int32, (rows, rows), 0) < lax.broadcasted_iota(
        jnp.int32, (rows, rows), 1
    )
    same = jnp.where(jnp.logical_and(across == down, earlier), 1.0, 0.0)
    rank = jnp.sum(same, axis=0, keepdims=True).astype(jnp.int32)
    return rank * groups + target


def plan_kernel(groups, contexts, dest_ref, out_ref):
    rows = dest_ref.shape[1]
    dest = dest_ref[...]
    slot = slot_of_rows(dest, groups, contexts, rows)
    local = (dest % rows + 1).astype(jnp.float32)
    held = jnp.where(iota((groups, rows), 0) == slot % groups, local, 0.0)
    lanes = (iota((HDIM, rows), 0) == slot // groups).astype(jnp.bfloat16)
    table = matmul_nt(held.astype(jnp.bfloat16), lanes).astype(jnp.int32)
    base = lax.axis_index("ctx") * rows
    out_ref[...] = jnp.where(table > 0, table + base, 0).reshape(out_ref.shape)


def pack_kernel(groups, contexts, proj_ref, cot_ref, dest_ref, out_ref):
    rows = proj_ref.shape[0]
    width = cot_ref.shape[1]
    part = width // contexts
    pieces = 4 * part // HDIM
    slot = slot_of_rows(dest_ref[...], groups, contexts, rows)
    slots = SLOTS * groups
    pick = (lax.broadcasted_iota(jnp.int32, (slots, rows), 0) == slot).astype(jnp.bfloat16)
    swap = swap_matrix(pieces)
    for share in range(contexts):
        begin = share * part
        picked = [
            matmul(pick, block).astype(jnp.bfloat16)
            for block in (
                proj_ref[:, begin : begin + part],
                proj_ref[:, width + begin : width + begin + part],
                proj_ref[:, 2 * width + begin : 2 * width + begin + part],
                cot_ref[:, begin : begin + part],
            )
        ]
        picked = jnp.concatenate(picked, axis=1)
        for rank in range(SLOTS):
            chunks = []
            for first in range(rank * groups, (rank + 1) * groups, pieces):
                chunks.append(
                    jnp.concatenate(
                        [
                            picked[first : first + pieces, j * HDIM : (j + 1) * HDIM]
                            for j in range(pieces)
                        ],
                        axis=0,
                    )
                )
            swapped = matmul(swap, jnp.concatenate(chunks, axis=1)).astype(jnp.bfloat16)
            for at in range(groups // pieces):
                out_ref[
                    at * pieces : (at + 1) * pieces, share, rank * pieces : (rank + 1) * pieces, :
                ] = swapped[:, at * HDIM : (at + 1) * HDIM].reshape(pieces, pieces, HDIM)


def unpack_kernel(groups, contexts, in_ref, dest_ref, attended_ref, grad_ref):
    rows, width = attended_ref.shape
    part = width // contexts
    pieces = 4 * part // HDIM
    slot = slot_of_rows(dest_ref[...], groups, contexts, rows)
    slots = SLOTS * groups
    slot_down = jnp.transpose(jnp.broadcast_to(slot.astype(jnp.float32), (rows, rows)))[:, :1]
    pick = (
        lax.broadcasted_iota(jnp.int32, (rows, slots), 1) == slot_down.astype(jnp.int32)
    ).astype(jnp.bfloat16)
    swap = swap_matrix(pieces)
    for share in range(contexts):
        stacked = []
        for rank in range(SLOTS):
            chunks = jnp.concatenate(
                [
                    in_ref[
                        first : first + pieces, share, rank * pieces : (rank + 1) * pieces, :
                    ].reshape(pieces * pieces, HDIM)
                    for first in range(0, groups, pieces)
                ],
                axis=1,
            )
            swapped = matmul(swap, chunks).astype(jnp.bfloat16)
            for at in range(groups // pieces):
                stacked.append(
                    jnp.concatenate(
                        [
                            swapped[j * pieces : (j + 1) * pieces, at * HDIM : (at + 1) * HDIM]
                            for j in range(pieces)
                        ],
                        axis=1,
                    )
                )
        result = matmul(pick, jnp.concatenate(stacked, axis=0)).astype(jnp.bfloat16)
        begin = share * part
        attended_ref[:, begin : begin + part] = result[:, :part]
        for t in range(3):
            grad_ref[:, t * width + begin : t * width + begin + part] = result[
                :, (t + 1) * part : (t + 2) * part
            ]


def attend_kernel(group_rows, in_ref, place_ref, lengths_ref, out_ref, slot_ref, back_ref):
    devices = place_ref.shape[0]
    pieces = in_ref.shape[1] // SLOTS
    heads = pieces // 4
    slots = SLOTS * devices
    swap = swap_matrix(pieces)

    downs, acrosses = [], []
    for rank in range(SLOTS):
        down = place_ref[:, rank : rank + 1] - 1
        downs.append(down)
        spread = jnp.broadcast_to(down.astype(jnp.float32), (devices, HDIM))
        acrosses.append(jnp.transpose(spread)[:1, :])
    place_down = jnp.concatenate(downs, axis=0)
    place_across = jnp.concatenate(acrosses, axis=1).astype(jnp.int32)
    gather = (
        lax.broadcasted_iota(jnp.int32, (group_rows, slots), 0) == place_across
    ).astype(jnp.bfloat16)
    scatter = (
        lax.broadcasted_iota(jnp.int32, (slots, group_rows), 1) == place_down
    ).astype(jnp.bfloat16)

    for rank in range(SLOTS):
        for first in range(0, devices, 4 * pieces):
            chunks = jnp.concatenate(
                [
                    in_ref[
                        first + at * pieces : first + (at + 1) * pieces,
                        rank * pieces : (rank + 1) * pieces,
                        :,
                    ].reshape(pieces * pieces, HDIM)
                    for at in range(4)
                ],
                axis=1,
            )
            swapped = matmul(swap, chunks).astype(jnp.bfloat16)
            for at in range(4):
                begin = rank * devices + first + at * pieces
                for j in range(pieces):
                    slot_ref[begin : begin + pieces, j * HDIM : (j + 1) * HDIM] = swapped[
                        j * pieces : (j + 1) * pieces, at * HDIM : (at + 1) * HDIM
                    ]

    end0 = lengths_ref[0, 0]
    end1 = end0 + lengths_ref[0, 1]
    end2 = end1 + lengths_ref[0, 2]

    def segment(shape, axis):
        position = lax.broadcasted_iota(jnp.int32, shape, axis)
        return (
            (position >= end0).astype(jnp.int32)
            + (position >= end1).astype(jnp.int32)
            + (position >= end2).astype(jnp.int32)
        )

    bias = jnp.where(
        segment((group_rows, group_rows), 0) == segment((group_rows, group_rows), 1), 0.0, LOWEST
    )
    scale = 1.0 / math.sqrt(HDIM)
    for head in range(heads):
        query, key, value, cotangent = [
            matmul(
                gather, slot_ref[:, (t * heads + head) * HDIM : (t * heads + head + 1) * HDIM]
            ).astype(jnp.bfloat16)
            for t in range(4)
        ]
        scores = matmul_nt(key, query) * (scale * math.log2(math.e)) + bias
        top = jnp.max(scores, axis=0, keepdims=True)
        powers = jnp.exp2(scores - top)
        total = jnp.sum(powers, axis=0, keepdims=True)
        exact = powers * (1.0 / total)
        weights = exact.astype(jnp.bfloat16)
        mixed = matmul(jnp.transpose(value), weights)
        drift = jnp.sum(
            jnp.transpose(cotangent).astype(jnp.float32) * mixed, axis=0, keepdims=True
        )
        pulls = matmul_nt(value, cotangent)
        slopes = (exact * ((pulls - drift) * scale)).astype(jnp.bfloat16)
        query_grad = matmul(jnp.transpose(key), slopes)
        key_grad = matmul(slopes, query)
        value_grad = matmul(weights, cotangent)
        by_query = jnp.concatenate([mixed, query_grad], axis=0).astype(jnp.bfloat16)
        by_key = jnp.concatenate([key_grad, value_grad], axis=1).astype(jnp.bfloat16)
        results = (matmul_nt(scatter, by_query), matmul(scatter, by_key))
        for t in range(4):
            j = t * heads + head
            back_ref[:, j * HDIM : (j + 1) * HDIM] = results[t // 2][
                :, t % 2 * HDIM : (t % 2 + 1) * HDIM
            ].astype(jnp.bfloat16)

    for rank in range(SLOTS):
        for first in range(0, devices, 4 * pieces):
            chunks = []
            for at in range(4):
                begin = rank * devices + first + at * pieces
                chunks.append(
                    jnp.concatenate(
                        [
                            back_ref[begin : begin + pieces, j * HDIM : (j + 1) * HDIM]
                            for j in range(pieces)
                        ],
                        axis=0,
                    )
                )
            swapped = matmul(swap, jnp.concatenate(chunks, axis=1)).astype(jnp.bfloat16)
            for at in range(4):
                out_ref[
                    first + at * pieces : first + (at + 1) * pieces,
                    rank * pieces : (rank + 1) * pieces,
                    :,
                ] = swapped[:, at * HDIM : (at + 1) * HDIM].reshape(pieces, pieces, HDIM)


def on_device(projected, out_grad, dest_row, lengths):
    rows, width = out_grad.shape
    groups = lax.axis_size("dp")
    contexts = lax.axis_size("ctx")
    devices = groups * contexts
    part = width // contexts
    pieces = 4 * part // HDIM
    everyone = ("dp", "ctx")
    params = pltpu.CompilerParams(vmem_limit_bytes=VMEM_LIMIT)
    whole = pl.BlockSpec(memory_space=pltpu.VMEM)

    dest = dest_row.reshape(1, rows)
    plan = pl.pallas_call(
        lambda *refs: plan_kernel(groups, contexts, *refs),
        out_shape=jax.ShapeDtypeStruct((groups, 1, HDIM), jnp.int32),
        in_specs=[whole],
        out_specs=whole,
        compiler_params=params,
        name="plan",
    )(dest)
    plan = lax.all_to_all(plan, "dp", 0, 0, tiled=True)

    sent = pl.pallas_call(
        lambda *refs: pack_kernel(groups, contexts, *refs),
        out_shape=jax.ShapeDtypeStruct((groups, contexts, SLOTS * pieces, HDIM), jnp.bfloat16),
        in_specs=[whole] * 3,
        out_specs=whole,
        compiler_params=params,
        name="pack",
    )(projected, out_grad, dest)
    arrived = lax.all_to_all(
        sent.reshape(devices, SLOTS * pieces, HDIM), everyone, 0, 0, tiled=True
    )
    places = lax.all_gather(plan, "ctx", axis=1, tiled=True).reshape(devices, HDIM)
    answers = pl.pallas_call(
        lambda *refs: attend_kernel(rows * contexts, *refs),
        out_shape=jax.ShapeDtypeStruct((devices, SLOTS * pieces, HDIM), jnp.bfloat16),
        in_specs=[whole, whole, pl.BlockSpec(memory_space=pltpu.SMEM)],
        out_specs=whole,
        scratch_shapes=[
            pltpu.VMEM((SLOTS * devices, pieces * HDIM), jnp.bfloat16),
            pltpu.VMEM((SLOTS * devices, pieces * HDIM), jnp.bfloat16),
        ],
        compiler_params=params,
        name="attend",
    )(arrived, places, lengths)
    returned = lax.all_to_all(answers, everyone, 0, 0, tiled=True)
    return pl.pallas_call(
        lambda *refs: unpack_kernel(groups, contexts, *refs),
        out_shape=(
            jax.ShapeDtypeStruct((rows, width), jnp.bfloat16),
            jax.ShapeDtypeStruct((rows, 3 * width), jnp.bfloat16),
        ),
        in_specs=[whole] * 2,
        out_specs=(whole, whole),
        compiler_params=params,
        name="unpack",
    )(returned.reshape(groups, contexts, SLOTS * pieces, HDIM), dest)


def solution(mesh):
    placed = (P(("dp", "ctx"), None), P(("dp", "ctx"), None), P(("dp", "ctx")), P("dp", None))
    return jax.shard_map(
        on_device,
        mesh=mesh,
        in_specs=placed,
        out_specs=(P(("dp", "ctx"), None), P(("dp", "ctx"), None)),
        check_vma=False,
    )
```

```python
import math

import jax
import jax.numpy as jnp
from jax import lax
from jax.experimental import pallas as pl
from jax.experimental.pallas import tpu as pltpu
from jax.sharding import Mesh, PartitionSpec as P

DP = ("z", "x", "core")
HDIM = 128
SLOTS = 3
LOWEST = -1e30
MIB = 1024 * 1024


def swap_matrix(side):
    rows = lax.broadcasted_iota(jnp.int32, (side * side, side * side), 0)
    cols = lax.broadcasted_iota(jnp.int32, (side * side, side * side), 1)
    partner = (rows % side) * side + rows // side
    return (cols == partner).astype(jnp.bfloat16)


def iota(shape, axis):
    return lax.broadcasted_iota(jnp.int32, shape, axis)


def matmul(left, right):
    return jnp.dot(left, right, preferred_element_type=jnp.float32)


def matmul_nt(left, right):
    return lax.dot_general(
        left, right, (((1,), (1,)), ((), ())), preferred_element_type=jnp.float32
    )


def slot_of_rows(dest, groups, contexts, rows):
    target = dest // (rows * contexts)
    across = jnp.broadcast_to(target.astype(jnp.float32), (rows, rows))
    down = jnp.transpose(across)
    earlier = lax.broadcasted_iota(jnp.int32, (rows, rows), 0) < lax.broadcasted_iota(
        jnp.int32, (rows, rows), 1
    )
    same = jnp.where(jnp.logical_and(across == down, earlier), 1.0, 0.0)
    rank = jnp.sum(same, axis=0, keepdims=True).astype(jnp.int32)
    return rank * groups + target


def plan_kernel(groups, contexts, dest_ref, out_ref):
    rows = dest_ref.shape[1]
    planes = out_ref.shape[0]
    spots = groups // planes
    dest = dest_ref[...]
    slot = slot_of_rows(dest, groups, contexts, rows)
    group, rank = slot % groups, slot // groups
    local = (dest % rows + 1).astype(jnp.float32)
    held = jnp.where(iota((planes, rows), 0) == group // spots, local, 0.0)
    lanes = (iota((HDIM, rows), 0) == rank * spots + group % spots).astype(jnp.bfloat16)
    table = matmul_nt(held.astype(jnp.bfloat16), lanes).astype(jnp.int32)
    base = lax.axis_index("ctx") * rows
    out_ref[...] = jnp.where(table > 0, table + base, 0).reshape(out_ref.shape)


def pack_kernel(groups, contexts, proj_ref, cot_ref, dest_ref, out_ref, spread_ref, gone_ref, sem):
    rows = proj_ref.shape[0]
    width = cot_ref.shape[1]
    part = width // contexts
    pieces = 4 * part // HDIM
    slot = slot_of_rows(dest_ref[...], groups, contexts, rows)
    slots = SLOTS * groups
    pick = (iota((slots, rows), 0) == slot % groups * SLOTS + slot // groups).astype(jnp.bfloat16)
    departures = []
    for share in range(contexts):
        begin = share * part
        for t in range(4):
            source, at = (proj_ref, t * width + begin) if t < 3 else (cot_ref, begin)
            picked = matmul(pick, source[:, at : at + part])
            for k in range(part // HDIM):
                j = t * (part // HDIM) + k
                spread_ref[share % 2, pl.ds(j, slots, stride=pieces), :] = picked[
                    :, k * HDIM : (k + 1) * HDIM
                ]
        gone_ref[share] = (
            spread_ref[share % 2].astype(jnp.bfloat16).reshape(groups, SLOTS * pieces, HDIM)
        )
        departures.append(
            pltpu.make_async_copy(gone_ref.at[share], out_ref.at[:, share], sem.at[share])
        )
        departures[-1].start()
    for departure in departures:
        departure.wait()


def unpack_kernel(
    groups,
    contexts,
    in_ref,
    dest_ref,
    attended_ref,
    grad_ref,
    here_ref,
    gone_ref,
    in_sem,
    out_sem,
):
    rows, width = attended_ref.shape
    part = width // contexts
    pieces = 4 * part // HDIM
    arrivals = []
    for share in range(contexts):
        arrivals.append(
            pltpu.make_async_copy(in_ref.at[:, share], here_ref.at[share], in_sem.at[share])
        )
        arrivals[-1].start()
    slot = slot_of_rows(dest_ref[...], groups, contexts, rows)
    slots = SLOTS * groups
    slot_down = jnp.transpose(jnp.broadcast_to(slot.astype(jnp.float32), (rows, rows)))[:, :1]
    pick = (iota((rows, slots), 1) == slot_down.astype(jnp.int32)).astype(jnp.bfloat16)
    swap = swap_matrix(pieces)
    departures = []
    for share in range(contexts):
        arrivals[share].wait()
        stacked = []
        for rank in range(SLOTS):
            chunks = jnp.concatenate(
                [
                    here_ref[
                        share, first : first + pieces, rank * pieces : (rank + 1) * pieces, :
                    ].reshape(pieces * pieces, HDIM)
                    for first in range(0, groups, pieces)
                ],
                axis=1,
            )
            swapped = matmul(swap, chunks).astype(jnp.bfloat16)
            for at in range(groups // pieces):
                stacked.append(
                    jnp.concatenate(
                        [
                            swapped[j * pieces : (j + 1) * pieces, at * HDIM : (at + 1) * HDIM]
                            for j in range(pieces)
                        ],
                        axis=1,
                    )
                )
        result = matmul(pick, jnp.concatenate(stacked, axis=0)).astype(jnp.bfloat16)
        begin = share * part
        for t in range(4):
            gone_ref[share, t] = result[:, t * part : (t + 1) * part]
            target, at = (grad_ref, (t - 1) * width + begin) if t else (attended_ref, begin)
            target = target.at[:, pl.ds(at, part)]
            departures.append(
                pltpu.make_async_copy(gone_ref.at[share, t], target, out_sem.at[share, t])
            )
            departures[-1].start()
    for departure in departures:
        departure.wait()


def attend_kernel(
    in_ref,
    place_ref,
    lengths_ref,
    out_ref,
    here_ref,
    slot_ref,
    row_ref,
    back_ref,
    gone_ref,
    in_sem,
    out_sem,
):
    groups, contexts, lines, _ = in_ref.shape
    pieces = lines // SLOTS
    heads = pieces // 4
    rows = row_ref.shape[0] // contexts
    spots = lax.axis_size("x") * lax.axis_size("core")
    arrivals = []
    for context in range(contexts):
        arrivals.append(
            pltpu.make_async_copy(
                in_ref.at[:, context], here_ref.at[context], in_sem.at[context]
            )
        )
        arrivals[-1].start()
    swap = swap_matrix(pieces)

    scatters, gathers = [], []
    for context in range(contexts):
        downs, acrosses = [], []
        for rank in range(SLOTS):
            lane = rank * spots + lax.axis_index("x") * lax.axis_size("core")
            lane = lane + lax.axis_index("core")
            place = place_ref[context].astype(jnp.float32)
            place = jnp.where(iota((groups, HDIM), 1) == lane, place, 0.0)
            down = jnp.sum(place, axis=1, keepdims=True) - (context * rows + 1.0)
            downs.append(down.astype(jnp.int32))
            spread = jnp.broadcast_to(down, (groups, HDIM))
            acrosses.append(jnp.transpose(spread)[:1, :])
        place_down = jnp.concatenate(downs, axis=0)
        place_across = jnp.concatenate(acrosses, axis=1).astype(jnp.int32)
        slots = SLOTS * groups
        gathers.append((iota((rows, slots), 0) == place_across).astype(jnp.bfloat16))
        scatters.append((iota((slots, rows), 1) == place_down).astype(jnp.bfloat16))

    end0 = lengths_ref[0, 0]
    end1 = end0 + lengths_ref[0, 1]
    end2 = end1 + lengths_ref[0, 2]

    def segment(axis):
        position = iota((contexts * rows, contexts * rows), axis)
        return (
            (position >= end0).astype(jnp.int32)
            + (position >= end1).astype(jnp.int32)
            + (position >= end2).astype(jnp.int32)
        )

    bias = jnp.where(segment(0) == segment(1), 0.0, LOWEST)

    for context in range(contexts):
        arrivals[context].wait()
        for rank in range(SLOTS):
            chunks = jnp.concatenate(
                [
                    here_ref[
                        context, first : first + pieces, rank * pieces : (rank + 1) * pieces, :
                    ].reshape(pieces * pieces, HDIM)
                    for first in range(0, groups, pieces)
                ],
                axis=1,
            )
            swapped = matmul(swap, chunks).astype(jnp.bfloat16)
            for at in range(groups // pieces):
                begin = rank * groups + at * pieces
                for j in range(pieces):
                    slot_ref[context, begin : begin + pieces, j * HDIM : (j + 1) * HDIM] = swapped[
                        j * pieces : (j + 1) * pieces, at * HDIM : (at + 1) * HDIM
                    ]
        row_ref[context * rows : (context + 1) * rows, :] = matmul(
            gathers[context], slot_ref[context]
        ).astype(jnp.bfloat16)

    scale = 1.0 / math.sqrt(HDIM)
    for head in range(heads):
        query, key, value, cotangent = [
            row_ref[:, (t * heads + head) * HDIM : (t * heads + head + 1) * HDIM]
            for t in range(4)
        ]
        scores = matmul_nt(key, query) * (scale * math.log2(math.e)) + bias
        top = jnp.max(scores, axis=0, keepdims=True)
        powers = jnp.exp2(scores - top)
        total = jnp.sum(powers, axis=0, keepdims=True)
        exact = powers * (1.0 / total)
        weights = exact.astype(jnp.bfloat16)
        mixed = matmul(jnp.transpose(value), weights)
        drift = jnp.sum(
            jnp.transpose(cotangent).astype(jnp.float32) * mixed, axis=0, keepdims=True
        )
        pulls = matmul_nt(value, cotangent)
        slopes = (exact * ((pulls - drift) * scale)).astype(jnp.bfloat16)
        query_grad = matmul(jnp.transpose(key), slopes)
        key_grad = matmul(slopes, query)
        value_grad = matmul(weights, cotangent)
        by_query = jnp.concatenate([mixed, query_grad], axis=0).astype(jnp.bfloat16)
        by_key = jnp.concatenate([key_grad, value_grad], axis=1).astype(jnp.bfloat16)
        for context in range(contexts):
            span = slice(context * rows, (context + 1) * rows)
            results = (
                matmul_nt(scatters[context], by_query[:, span]),
                matmul(scatters[context], by_key[span, :]),
            )
            for t in range(4):
                j = t * heads + head
                back_ref[context, :, j * HDIM : (j + 1) * HDIM] = results[t // 2][
                    :, t % 2 * HDIM : (t % 2 + 1) * HDIM
                ].astype(jnp.bfloat16)

    departures = []
    for context in range(contexts):
        for rank in range(SLOTS):
            chunks = []
            for first in range(rank * groups, (rank + 1) * groups, pieces):
                chunks.append(
                    jnp.concatenate(
                        [
                            back_ref[context, first : first + pieces, j * HDIM : (j + 1) * HDIM]
                            for j in range(pieces)
                        ],
                        axis=0,
                    )
                )
            swapped = matmul(swap, jnp.concatenate(chunks, axis=1)).astype(jnp.bfloat16)
            for at in range(groups // pieces):
                gone_ref[
                    context, at * pieces : (at + 1) * pieces, rank * pieces : (rank + 1) * pieces, :
                ] = swapped[:, at * HDIM : (at + 1) * HDIM].reshape(pieces, pieces, HDIM)
        departures.append(
            pltpu.make_async_copy(
                gone_ref.at[context], out_ref.at[:, context], out_sem.at[context]
            )
        )
        departures[-1].start()
    for departure in departures:
        departure.wait()


def call_pack(groups, contexts, projected, out_grad, dest):
    lanes = 4 * out_grad.shape[1] // contexts
    pieces = lanes // HDIM
    whole = pl.BlockSpec(memory_space=pltpu.VMEM)
    return pl.pallas_call(
        lambda *refs: pack_kernel(groups, contexts, *refs),
        out_shape=jax.ShapeDtypeStruct((groups, contexts, SLOTS * pieces, HDIM), jnp.bfloat16),
        in_specs=[whole] * 3,
        out_specs=pl.BlockSpec(memory_space=pl.ANY),
        scratch_shapes=[
            pltpu.VMEM((2, SLOTS * groups * pieces, HDIM), jnp.float32),
            pltpu.VMEM((contexts, groups, SLOTS * pieces, HDIM), jnp.bfloat16),
            pltpu.SemaphoreType.DMA((contexts,)),
        ],
        compiler_params=pltpu.CompilerParams(vmem_limit_bytes=56 * MIB),
        name="pack",
    )(projected, out_grad, dest)


def call_plan(groups, contexts, planes, dest):
    whole = pl.BlockSpec(memory_space=pltpu.VMEM)
    return pl.pallas_call(
        lambda *refs: plan_kernel(groups, contexts, *refs),
        out_shape=jax.ShapeDtypeStruct((planes, 1, HDIM), jnp.int32),
        in_specs=[whole],
        out_specs=whole,
        compiler_params=pltpu.CompilerParams(vmem_limit_bytes=8 * MIB),
        name="plan",
    )(dest)


def call_attend(contexts, rows, arrived, places, lengths):
    devices, lines, _ = arrived.shape
    groups = devices // contexts
    lanes = lines // SLOTS * HDIM
    whole = pl.BlockSpec(memory_space=pltpu.VMEM)
    far = pl.BlockSpec(memory_space=pl.ANY)
    blocks = pltpu.VMEM((contexts, groups, lines, HDIM), jnp.bfloat16)
    slots = pltpu.VMEM((contexts, SLOTS * groups, lanes), jnp.bfloat16)
    return pl.pallas_call(
        attend_kernel,
        out_shape=jax.ShapeDtypeStruct((groups, contexts, lines, HDIM), jnp.bfloat16),
        in_specs=[far, whole, pl.BlockSpec(memory_space=pltpu.SMEM)],
        out_specs=far,
        scratch_shapes=[
            blocks,
            slots,
            pltpu.VMEM((contexts * rows, lanes), jnp.bfloat16),
            slots,
            blocks,
            pltpu.SemaphoreType.DMA((contexts,)),
            pltpu.SemaphoreType.DMA((contexts,)),
        ],
        compiler_params=pltpu.CompilerParams(vmem_limit_bytes=36 * MIB),
        name="attend",
    )(arrived.reshape(groups, contexts, lines, HDIM), places, lengths)


def call_unpack(groups, contexts, returned, dest):
    rows = dest.shape[1]
    lines = returned.shape[2]
    part = lines // (SLOTS * 4) * HDIM
    width = contexts * part
    whole = pl.BlockSpec(memory_space=pltpu.VMEM)
    far = pl.BlockSpec(memory_space=pl.ANY)
    return pl.pallas_call(
        lambda *refs: unpack_kernel(groups, contexts, *refs),
        out_shape=(
            jax.ShapeDtypeStruct((rows, width), jnp.bfloat16),
            jax.ShapeDtypeStruct((rows, 3 * width), jnp.bfloat16),
        ),
        in_specs=[far, whole],
        out_specs=(far, far),
        scratch_shapes=[
            pltpu.VMEM((contexts, groups, lines, HDIM), jnp.bfloat16),
            pltpu.VMEM((contexts, 4, rows, part), jnp.bfloat16),
            pltpu.SemaphoreType.DMA((contexts,)),
            pltpu.SemaphoreType.DMA((contexts, 4)),
        ],
        compiler_params=pltpu.CompilerParams(vmem_limit_bytes=20 * MIB),
        name="unpack",
    )(returned, dest)


def on_device(projected, out_grad, dest_row, lengths):
    rows = out_grad.shape[0]
    planes, contexts = lax.axis_size("z"), lax.axis_size("ctx")
    groups = lax.axis_size(DP)
    everyone = DP + ("ctx",)
    dest = dest_row.reshape(1, rows)

    plan = call_plan(groups, contexts, planes, dest)
    plan = lax.all_to_all(plan, "z", 0, 0, tiled=True).reshape(planes, HDIM)
    sent = call_pack(groups, contexts, projected, out_grad, dest)
    lines = sent.shape[2]
    arrived = lax.all_to_all(sent.reshape(-1, lines, HDIM), everyone, 0, 0, tiled=True)
    places = plan
    for axis in ("ctx", "core", "x"):
        places = lax.all_gather(places, axis, axis=0)
    places = jnp.transpose(places, (2, 3, 0, 1, 4)).reshape(contexts, groups, HDIM)
    answers = call_attend(contexts, rows, arrived, places, lengths)
    returned = lax.all_to_all(
        answers.reshape(-1, lines, HDIM), everyone, 0, 0, tiled=True
    )
    return call_unpack(
        groups, contexts, returned.reshape(groups, contexts, lines, HDIM), dest
    )


def solution(mesh):
    parts = Mesh(mesh.devices.reshape(8, 4, 2, -1), DP + ("ctx",))
    everyone = DP + ("ctx",)
    return jax.shard_map(
        on_device,
        mesh=parts,
        in_specs=(P(everyone, None), P(everyone, None), P(everyone), P(DP, None)),
        out_specs=(P(everyone, None), P(everyone, None)),
        check_vma=False,
    )
```

```python
import math

import jax
import jax.numpy as jnp
from jax import lax
from jax.experimental import pallas as pl
from jax.experimental.pallas import tpu as pltpu
from jax.sharding import Mesh, PartitionSpec as P

DP = ("z", "x", "core")
HDIM = 128
SLOTS = 3
LOWEST = -1e30
MIB = 1024 * 1024


def swap_matrix(side):
    rows = lax.broadcasted_iota(jnp.int32, (side * side, side * side), 0)
    cols = lax.broadcasted_iota(jnp.int32, (side * side, side * side), 1)
    partner = (rows % side) * side + rows // side
    return (cols == partner).astype(jnp.bfloat16)


def iota(shape, axis):
    return lax.broadcasted_iota(jnp.int32, shape, axis)


def matmul(left, right):
    return jnp.dot(left, right, preferred_element_type=jnp.float32)


def matmul_nt(left, right):
    return lax.dot_general(
        left, right, (((1,), (1,)), ((), ())), preferred_element_type=jnp.float32
    )


def slot_of_rows(dest, groups, contexts, rows):
    target = dest // (rows * contexts)
    across = jnp.broadcast_to(target.astype(jnp.float32), (rows, rows))
    down = jnp.transpose(across)
    earlier = lax.broadcasted_iota(jnp.int32, (rows, rows), 0) < lax.broadcasted_iota(
        jnp.int32, (rows, rows), 1
    )
    same = jnp.where(jnp.logical_and(across == down, earlier), 1.0, 0.0)
    rank = jnp.sum(same, axis=0, keepdims=True).astype(jnp.int32)
    return rank * groups + target


def plan_kernel(groups, contexts, dest_ref, out_ref):
    rows = dest_ref.shape[1]
    planes = out_ref.shape[0]
    spots = groups // planes
    dest = dest_ref[...]
    slot = slot_of_rows(dest, groups, contexts, rows)
    group, rank = slot % groups, slot // groups
    local = (dest % rows + 1).astype(jnp.float32)
    held = jnp.where(iota((planes, rows), 0) == group // spots, local, 0.0)
    lanes = (iota((HDIM, rows), 0) == rank * spots + group % spots).astype(jnp.bfloat16)
    table = matmul_nt(held.astype(jnp.bfloat16), lanes).astype(jnp.int32)
    base = lax.axis_index("ctx") * rows
    out_ref[...] = jnp.where(table > 0, table + base, 0).reshape(out_ref.shape)


def pack_kernel(groups, contexts, proj_ref, cot_ref, dest_ref, out_ref, spread_ref, gone_ref, sem):
    rows = proj_ref.shape[0]
    width = cot_ref.shape[1]
    part = width // contexts
    pieces = 4 * part // HDIM
    slot = slot_of_rows(dest_ref[...], groups, contexts, rows)
    slots = SLOTS * groups
    pick = (iota((slots, rows), 0) == slot % groups * SLOTS + slot // groups).astype(jnp.bfloat16)
    departures = []
    for share in range(contexts):
        begin = share * part
        for t in range(4):
            source, at = (proj_ref, t * width + begin) if t < 3 else (cot_ref, begin)
            picked = matmul(pick, source[:, at : at + part])
            for k in range(part // HDIM):
                j = t * (part // HDIM) + k
                spread_ref[share % 2, pl.ds(j, slots, stride=pieces), :] = picked[
                    :, k * HDIM : (k + 1) * HDIM
                ]
        gone_ref[share] = (
            spread_ref[share % 2].astype(jnp.bfloat16).reshape(groups, SLOTS * pieces, HDIM)
        )
        departures.append(
            pltpu.make_async_copy(gone_ref.at[share], out_ref.at[:, share], sem.at[share])
        )
        departures[-1].start()
    for departure in departures:
        departure.wait()


def unpack_kernel(
    groups,
    contexts,
    in_ref,
    dest_ref,
    attended_ref,
    grad_ref,
    gone_ref,
    out_sem,
):
    rows, width = attended_ref.shape
    part = width // contexts
    pieces = 4 * part // HDIM
    slot = slot_of_rows(dest_ref[...], groups, contexts, rows)
    slots = SLOTS * groups
    slot_down = jnp.transpose(jnp.broadcast_to(slot.astype(jnp.float32), (rows, rows)))[:, :1]
    pick = (iota((rows, slots), 1) == slot_down.astype(jnp.int32)).astype(jnp.bfloat16)
    swap = swap_matrix(pieces)
    departures = []
    for share in range(contexts):
        stacked = []
        for rank in range(SLOTS):
            chunks = jnp.concatenate(
                [
                    in_ref[
                        first : first + pieces, share, rank * pieces : (rank + 1) * pieces, :
                    ].reshape(pieces * pieces, HDIM)
                    for first in range(0, groups, pieces)
                ],
                axis=1,
            )
            swapped = matmul(swap, chunks).astype(jnp.bfloat16)
            for at in range(groups // pieces):
                stacked.append(
                    jnp.concatenate(
                        [
                            swapped[j * pieces : (j + 1) * pieces, at * HDIM : (at + 1) * HDIM]
                            for j in range(pieces)
                        ],
                        axis=1,
                    )
                )
        result = matmul(pick, jnp.concatenate(stacked, axis=0)).astype(jnp.bfloat16)
        begin = share * part
        for t in range(4):
            gone_ref[share, t] = result[:, t * part : (t + 1) * part]
            target, at = (grad_ref, (t - 1) * width + begin) if t else (attended_ref, begin)
            target = target.at[:, pl.ds(at, part)]
            departures.append(
                pltpu.make_async_copy(gone_ref.at[share, t], target, out_sem.at[share, t])
            )
            departures[-1].start()
    for departure in departures:
        departure.wait()


def attend_kernel(
    in_ref,
    place_ref,
    lengths_ref,
    out_ref,
    slot_ref,
    row_ref,
    back_ref,
    gone_ref,
    out_sem,
):
    groups, contexts, lines, _ = in_ref.shape
    pieces = lines // SLOTS
    heads = pieces // 4
    rows = row_ref.shape[0] // contexts
    spots = lax.axis_size("x") * lax.axis_size("core")
    swap = swap_matrix(pieces)

    scatters, gathers = [], []
    for context in range(contexts):
        downs, acrosses = [], []
        for rank in range(SLOTS):
            lane = rank * spots + lax.axis_index("x") * lax.axis_size("core")
            lane = lane + lax.axis_index("core")
            place = place_ref[context].astype(jnp.float32)
            place = jnp.where(iota((groups, HDIM), 1) == lane, place, 0.0)
            down = jnp.sum(place, axis=1, keepdims=True) - (context * rows + 1.0)
            downs.append(down.astype(jnp.int32))
            spread = jnp.broadcast_to(down, (groups, HDIM))
            acrosses.append(jnp.transpose(spread)[:1, :])
        place_down = jnp.concatenate(downs, axis=0)
        place_across = jnp.concatenate(acrosses, axis=1).astype(jnp.int32)
        slots = SLOTS * groups
        gathers.append((iota((rows, slots), 0) == place_across).astype(jnp.bfloat16))
        scatters.append((iota((slots, rows), 1) == place_down).astype(jnp.bfloat16))

    end0 = lengths_ref[0, 0]
    end1 = end0 + lengths_ref[0, 1]
    end2 = end1 + lengths_ref[0, 2]

    def segment(axis):
        position = iota((contexts * rows, contexts * rows), axis)
        return (
            (position >= end0).astype(jnp.int32)
            + (position >= end1).astype(jnp.int32)
            + (position >= end2).astype(jnp.int32)
        )

    bias = jnp.where(segment(0) == segment(1), 0.0, LOWEST)

    for context in range(contexts):
        for rank in range(SLOTS):
            chunks = jnp.concatenate(
                [
                    in_ref[
                        first : first + pieces, context, rank * pieces : (rank + 1) * pieces, :
                    ].reshape(pieces * pieces, HDIM)
                    for first in range(0, groups, pieces)
                ],
                axis=1,
            )
            swapped = matmul(swap, chunks).astype(jnp.bfloat16)
            for at in range(groups // pieces):
                begin = rank * groups + at * pieces
                for j in range(pieces):
                    slot_ref[context, begin : begin + pieces, j * HDIM : (j + 1) * HDIM] = swapped[
                        j * pieces : (j + 1) * pieces, at * HDIM : (at + 1) * HDIM
                    ]
        row_ref[context * rows : (context + 1) * rows, :] = matmul(
            gathers[context], slot_ref[context]
        ).astype(jnp.bfloat16)

    scale = 1.0 / math.sqrt(HDIM)
    for head in range(heads):
        query, key, value, cotangent = [
            row_ref[:, (t * heads + head) * HDIM : (t * heads + head + 1) * HDIM]
            for t in range(4)
        ]
        scores = matmul_nt(key, query) * (scale * math.log2(math.e)) + bias
        top = jnp.max(scores, axis=0, keepdims=True)
        powers = jnp.exp2(scores - top)
        total = jnp.sum(powers, axis=0, keepdims=True)
        exact = powers * (1.0 / total)
        weights = exact.astype(jnp.bfloat16)
        mixed = matmul(jnp.transpose(value), weights)
        drift = jnp.sum(
            jnp.transpose(cotangent).astype(jnp.float32) * mixed, axis=0, keepdims=True
        )
        pulls = matmul_nt(value, cotangent)
        slopes = (exact * ((pulls - drift) * scale)).astype(jnp.bfloat16)
        query_grad = matmul(jnp.transpose(key), slopes)
        key_grad = matmul(slopes, query)
        value_grad = matmul(weights, cotangent)
        by_query = jnp.concatenate([mixed, query_grad], axis=0).astype(jnp.bfloat16)
        by_key = jnp.concatenate([key_grad, value_grad], axis=1).astype(jnp.bfloat16)
        for context in range(contexts):
            span = slice(context * rows, (context + 1) * rows)
            results = (
                matmul_nt(scatters[context], by_query[:, span]),
                matmul(scatters[context], by_key[span, :]),
            )
            for t in range(4):
                j = t * heads + head
                back_ref[context, :, j * HDIM : (j + 1) * HDIM] = results[t // 2][
                    :, t % 2 * HDIM : (t % 2 + 1) * HDIM
                ].astype(jnp.bfloat16)

    departures = []
    for context in range(contexts):
        for rank in range(SLOTS):
            chunks = []
            for first in range(rank * groups, (rank + 1) * groups, pieces):
                chunks.append(
                    jnp.concatenate(
                        [
                            back_ref[context, first : first + pieces, j * HDIM : (j + 1) * HDIM]
                            for j in range(pieces)
                        ],
                        axis=0,
                    )
                )
            swapped = matmul(swap, jnp.concatenate(chunks, axis=1)).astype(jnp.bfloat16)
            for at in range(groups // pieces):
                gone_ref[
                    context, at * pieces : (at + 1) * pieces, rank * pieces : (rank + 1) * pieces, :
                ] = swapped[:, at * HDIM : (at + 1) * HDIM].reshape(pieces, pieces, HDIM)
        departures.append(
            pltpu.make_async_copy(
                gone_ref.at[context], out_ref.at[:, context], out_sem.at[context]
            )
        )
        departures[-1].start()
    for departure in departures:
        departure.wait()


def call_pack(groups, contexts, projected, out_grad, dest):
    lanes = 4 * out_grad.shape[1] // contexts
    pieces = lanes // HDIM
    whole = pl.BlockSpec(memory_space=pltpu.VMEM)
    return pl.pallas_call(
        lambda *refs: pack_kernel(groups, contexts, *refs),
        out_shape=jax.ShapeDtypeStruct((groups, contexts, SLOTS * pieces, HDIM), jnp.bfloat16),
        in_specs=[whole] * 3,
        out_specs=pl.BlockSpec(memory_space=pl.ANY),
        scratch_shapes=[
            pltpu.VMEM((2, SLOTS * groups * pieces, HDIM), jnp.float32),
            pltpu.VMEM((contexts, groups, SLOTS * pieces, HDIM), jnp.bfloat16),
            pltpu.SemaphoreType.DMA((contexts,)),
        ],
        compiler_params=pltpu.CompilerParams(vmem_limit_bytes=56 * MIB),
        name="pack",
    )(projected, out_grad, dest)


def call_plan(groups, contexts, planes, dest):
    whole = pl.BlockSpec(memory_space=pltpu.VMEM)
    return pl.pallas_call(
        lambda *refs: plan_kernel(groups, contexts, *refs),
        out_shape=jax.ShapeDtypeStruct((planes, 1, HDIM), jnp.int32),
        in_specs=[whole],
        out_specs=whole,
        compiler_params=pltpu.CompilerParams(vmem_limit_bytes=8 * MIB),
        name="plan",
    )(dest)


def call_attend(contexts, rows, arrived, places, lengths):
    devices, lines, _ = arrived.shape
    groups = devices // contexts
    lanes = lines // SLOTS * HDIM
    whole = pl.BlockSpec(memory_space=pltpu.VMEM)
    far = pl.BlockSpec(memory_space=pl.ANY)
    blocks = pltpu.VMEM((contexts, groups, lines, HDIM), jnp.bfloat16)
    slots = pltpu.VMEM((contexts, SLOTS * groups, lanes), jnp.bfloat16)
    return pl.pallas_call(
        attend_kernel,
        out_shape=jax.ShapeDtypeStruct((groups, contexts, lines, HDIM), jnp.bfloat16),
        in_specs=[whole, whole, pl.BlockSpec(memory_space=pltpu.SMEM)],
        out_specs=far,
        scratch_shapes=[
            slots,
            pltpu.VMEM((contexts * rows, lanes), jnp.bfloat16),
            slots,
            blocks,
            pltpu.SemaphoreType.DMA((contexts,)),
        ],
        compiler_params=pltpu.CompilerParams(vmem_limit_bytes=36 * MIB),
        name="attend",
    )(arrived.reshape(groups, contexts, lines, HDIM), places, lengths)


def call_unpack(groups, contexts, returned, dest):
    rows = dest.shape[1]
    lines = returned.shape[2]
    part = lines // (SLOTS * 4) * HDIM
    width = contexts * part
    whole = pl.BlockSpec(memory_space=pltpu.VMEM)
    far = pl.BlockSpec(memory_space=pl.ANY)
    return pl.pallas_call(
        lambda *refs: unpack_kernel(groups, contexts, *refs),
        out_shape=(
            jax.ShapeDtypeStruct((rows, width), jnp.bfloat16),
            jax.ShapeDtypeStruct((rows, 3 * width), jnp.bfloat16),
        ),
        in_specs=[whole, whole],
        out_specs=(far, far),
        scratch_shapes=[
            pltpu.VMEM((contexts, 4, rows, part), jnp.bfloat16),
            pltpu.SemaphoreType.DMA((contexts, 4)),
        ],
        compiler_params=pltpu.CompilerParams(vmem_limit_bytes=20 * MIB),
        name="unpack",
    )(returned, dest)


def on_device(projected, out_grad, dest_row, lengths):
    rows = out_grad.shape[0]
    planes, contexts = lax.axis_size("z"), lax.axis_size("ctx")
    groups = lax.axis_size(DP)
    everyone = DP + ("ctx",)
    dest = dest_row.reshape(1, rows)

    plan = call_plan(groups, contexts, planes, dest)
    plan = lax.all_to_all(plan, "z", 0, 0, tiled=True).reshape(planes, HDIM)
    sent = call_pack(groups, contexts, projected, out_grad, dest)
    lines = sent.shape[2]
    arrived = lax.all_to_all(sent.reshape(-1, lines, HDIM), everyone, 0, 0, tiled=True)
    places = plan
    for axis in ("ctx", "core", "x"):
        places = lax.all_gather(places, axis, axis=0)
    places = jnp.transpose(places, (2, 3, 0, 1, 4)).reshape(contexts, groups, HDIM)
    answers = call_attend(contexts, rows, arrived, places, lengths)
    returned = lax.all_to_all(
        answers.reshape(-1, lines, HDIM), everyone, 0, 0, tiled=True
    )
    return call_unpack(
        groups, contexts, returned.reshape(groups, contexts, lines, HDIM), dest
    )


def solution(mesh):
    parts = Mesh(mesh.devices.reshape(8, 4, 2, -1), DP + ("ctx",))
    everyone = DP + ("ctx",)
    return jax.shard_map(
        on_device,
        mesh=parts,
        in_specs=(P(everyone, None), P(everyone, None), P(everyone), P(DP, None)),
        out_specs=(P(everyone, None), P(everyone, None)),
        check_vma=False,
    )
```

```python
import math

import jax
import jax.numpy as jnp
from jax import lax
from jax.experimental import pallas as pl
from jax.experimental.pallas import tpu as pltpu
from jax.sharding import Mesh, PartitionSpec as P

DP = ("z", "x", "core")
HDIM = 128
SLOTS = 3
LOWEST = -1e30
MIB = 1024 * 1024


def swap_matrix(side):
    rows = lax.broadcasted_iota(jnp.int32, (side * side, side * side), 0)
    cols = lax.broadcasted_iota(jnp.int32, (side * side, side * side), 1)
    partner = (rows % side) * side + rows // side
    return (cols == partner).astype(jnp.bfloat16)


def iota(shape, axis):
    return lax.broadcasted_iota(jnp.int32, shape, axis)


def matmul(left, right):
    return jnp.dot(left, right, preferred_element_type=jnp.float32)


def matmul_nt(left, right):
    return lax.dot_general(
        left, right, (((1,), (1,)), ((), ())), preferred_element_type=jnp.float32
    )


def slot_of_rows(dest, groups, contexts, rows):
    target = dest // (rows * contexts)
    across = jnp.broadcast_to(target.astype(jnp.float32), (rows, rows))
    down = jnp.transpose(across)
    earlier = lax.broadcasted_iota(jnp.int32, (rows, rows), 0) < lax.broadcasted_iota(
        jnp.int32, (rows, rows), 1
    )
    same = jnp.where(jnp.logical_and(across == down, earlier), 1.0, 0.0)
    rank = jnp.sum(same, axis=0, keepdims=True).astype(jnp.int32)
    return rank * groups + target


def plan_kernel(groups, contexts, dest_ref, out_ref):
    rows = dest_ref.shape[1]
    planes = out_ref.shape[0]
    spots = groups // planes
    dest = dest_ref[...]
    slot = slot_of_rows(dest, groups, contexts, rows)
    group, rank = slot % groups, slot // groups
    local = (dest % rows + 1).astype(jnp.float32)
    held = jnp.where(iota((planes, rows), 0) == group // spots, local, 0.0)
    lanes = (iota((HDIM, rows), 0) == rank * spots + group % spots).astype(jnp.bfloat16)
    table = matmul_nt(held.astype(jnp.bfloat16), lanes).astype(jnp.int32)
    base = lax.axis_index("ctx") * rows
    out_ref[...] = jnp.where(table > 0, table + base, 0).reshape(out_ref.shape)


def pack_kernel(groups, contexts, proj_ref, cot_ref, dest_ref, out_ref, spread_ref, gone_ref, sem):
    rows = proj_ref.shape[0]
    width = cot_ref.shape[1]
    part = width // contexts
    pieces = 4 * part // HDIM
    slot = slot_of_rows(dest_ref[...], groups, contexts, rows)
    slots = SLOTS * groups
    pick = (iota((slots, rows), 0) == slot).astype(jnp.bfloat16)
    swap = swap_matrix(pieces)
    departures = []
    for share in range(contexts):
        begin = share * part
        picked = []
        for t in range(4):
            source, at = (proj_ref, t * width + begin) if t < 3 else (cot_ref, begin)
            picked.append(matmul(pick, source[:, at : at + part]).astype(jnp.bfloat16))
        picked = jnp.concatenate(picked, axis=1)
        for rank in range(SLOTS):
            chunks = []
            for first in range(rank * groups, (rank + 1) * groups, pieces):
                chunks.append(
                    jnp.concatenate(
                        [
                            picked[first : first + pieces, j * HDIM : (j + 1) * HDIM]
                            for j in range(pieces)
                        ],
                        axis=0,
                    )
                )
            swapped = matmul(swap, jnp.concatenate(chunks, axis=1)).astype(jnp.bfloat16)
            for at in range(groups // pieces):
                gone_ref[
                    share, at * pieces : (at + 1) * pieces, rank * pieces : (rank + 1) * pieces, :
                ] = swapped[:, at * HDIM : (at + 1) * HDIM].reshape(pieces, pieces, HDIM)
        departures.append(
            pltpu.make_async_copy(gone_ref.at[share], out_ref.at[:, share], sem.at[share])
        )
        departures[-1].start()
    for departure in departures:
        departure.wait()


def unpack_kernel(
    groups,
    contexts,
    in_ref,
    dest_ref,
    attended_ref,
    grad_ref,
    gone_ref,
    out_sem,
):
    rows, width = attended_ref.shape
    part = width // contexts
    pieces = 4 * part // HDIM
    slot = slot_of_rows(dest_ref[...], groups, contexts, rows)
    slots = SLOTS * groups
    slot_down = jnp.transpose(jnp.broadcast_to(slot.astype(jnp.float32), (rows, rows)))[:, :1]
    pick = (iota((rows, slots), 1) == slot_down.astype(jnp.int32)).astype(jnp.bfloat16)
    swap = swap_matrix(pieces)
    departures = []
    for share in range(contexts):
        stacked = []
        for rank in range(SLOTS):
            chunks = jnp.concatenate(
                [
                    in_ref[
                        first : first + pieces, share, rank * pieces : (rank + 1) * pieces, :
                    ].reshape(pieces * pieces, HDIM)
                    for first in range(0, groups, pieces)
                ],
                axis=1,
            )
            swapped = matmul(swap, chunks).astype(jnp.bfloat16)
            for at in range(groups // pieces):
                stacked.append(
                    jnp.concatenate(
                        [
                            swapped[j * pieces : (j + 1) * pieces, at * HDIM : (at + 1) * HDIM]
                            for j in range(pieces)
                        ],
                        axis=1,
                    )
                )
        result = matmul(pick, jnp.concatenate(stacked, axis=0)).astype(jnp.bfloat16)
        begin = share * part
        for t in range(4):
            gone_ref[share, t] = result[:, t * part : (t + 1) * part]
            target, at = (grad_ref, (t - 1) * width + begin) if t else (attended_ref, begin)
            target = target.at[:, pl.ds(at, part)]
            departures.append(
                pltpu.make_async_copy(gone_ref.at[share, t], target, out_sem.at[share, t])
            )
            departures[-1].start()
    for departure in departures:
        departure.wait()


def prepare_kernel(rows, place_ref, lengths_ref, scatter_ref, bias_ref):
    contexts, groups, _ = place_ref.shape
    spots = lax.axis_size("x") * lax.axis_size("core")
    for context in range(contexts):
        downs = []
        for rank in range(SLOTS):
            lane = rank * spots + lax.axis_index("x") * lax.axis_size("core")
            lane = lane + lax.axis_index("core")
            place = place_ref[context].astype(jnp.float32)
            place = jnp.where(iota((groups, HDIM), 1) == lane, place, 0.0)
            down = jnp.sum(place, axis=1, keepdims=True) - (context * rows + 1.0)
            downs.append(down.astype(jnp.int32))
        place_down = jnp.concatenate(downs, axis=0)
        slots = SLOTS * groups
        scatter_ref[context] = (iota((slots, rows), 1) == place_down).astype(jnp.bfloat16)

    end0 = lengths_ref[0, 0]
    end1 = end0 + lengths_ref[0, 1]
    end2 = end1 + lengths_ref[0, 2]

    def segment(axis):
        position = iota((contexts * rows, contexts * rows), axis)
        return (
            (position >= end0).astype(jnp.int32)
            + (position >= end1).astype(jnp.int32)
            + (position >= end2).astype(jnp.int32)
        )

    bias_ref[...] = jnp.where(segment(0) == segment(1), 0.0, LOWEST)


def attend_kernel(
    in_ref,
    place_ref,
    scatter_hbm,
    bias_hbm,
    out_ref,
    slot_ref,
    row_ref,
    back_ref,
    gone_ref,
    bias_ref,
    scatter_ref,
    in_sem,
    out_sem,
):
    groups, contexts, lines, _ = in_ref.shape
    pieces = lines // SLOTS
    heads = pieces // 4
    rows = row_ref.shape[0] // contexts
    spots = lax.axis_size("x") * lax.axis_size("core")
    early = (
        pltpu.make_async_copy(bias_hbm, bias_ref, in_sem.at[0]),
        pltpu.make_async_copy(scatter_hbm, scatter_ref, in_sem.at[1]),
    )
    for copy in early:
        copy.start()
    swap = swap_matrix(pieces)
    gathers = []
    for context in range(contexts):
        acrosses = []
        for rank in range(SLOTS):
            lane = rank * spots + lax.axis_index("x") * lax.axis_size("core")
            lane = lane + lax.axis_index("core")
            place = place_ref[context].astype(jnp.float32)
            place = jnp.where(iota((groups, HDIM), 1) == lane, place, 0.0)
            down = jnp.sum(place, axis=1, keepdims=True) - (context * rows + 1.0)
            spread = jnp.broadcast_to(down, (groups, HDIM))
            acrosses.append(jnp.transpose(spread)[:1, :])
        place_across = jnp.concatenate(acrosses, axis=1).astype(jnp.int32)
        gathers.append(
            (iota((rows, SLOTS * groups), 0) == place_across).astype(jnp.bfloat16)
        )

    for context in range(contexts):
        for rank in range(SLOTS):
            chunks = jnp.concatenate(
                [
                    in_ref[
                        first : first + pieces, context, rank * pieces : (rank + 1) * pieces, :
                    ].reshape(pieces * pieces, HDIM)
                    for first in range(0, groups, pieces)
                ],
                axis=1,
            )
            swapped = matmul(swap, chunks).astype(jnp.bfloat16)
            for at in range(groups // pieces):
                begin = rank * groups + at * pieces
                for j in range(pieces):
                    slot_ref[context, begin : begin + pieces, j * HDIM : (j + 1) * HDIM] = swapped[
                        j * pieces : (j + 1) * pieces, at * HDIM : (at + 1) * HDIM
                    ]
        row_ref[context * rows : (context + 1) * rows, :] = matmul(
            gathers[context], slot_ref[context]
        ).astype(jnp.bfloat16)

    for copy in early:
        copy.wait()
    bias = bias_ref[...]
    scale = 1.0 / math.sqrt(HDIM)
    for head in range(heads):
        query, key, value, cotangent = [
            row_ref[:, (t * heads + head) * HDIM : (t * heads + head + 1) * HDIM]
            for t in range(4)
        ]
        scores = matmul_nt(key, query) * (scale * math.log2(math.e)) + bias
        top = jnp.max(scores, axis=0, keepdims=True)
        powers = jnp.exp2(scores - top)
        total = jnp.sum(powers, axis=0, keepdims=True)
        exact = powers * (1.0 / total)
        weights = exact.astype(jnp.bfloat16)
        mixed = matmul(jnp.transpose(value), weights)
        drift = jnp.sum(
            jnp.transpose(cotangent).astype(jnp.float32) * mixed, axis=0, keepdims=True
        )
        pulls = matmul_nt(value, cotangent)
        slopes = (exact * ((pulls - drift) * scale)).astype(jnp.bfloat16)
        query_grad = matmul(jnp.transpose(key), slopes)
        key_grad = matmul(slopes, query)
        value_grad = matmul(weights, cotangent)
        by_query = jnp.concatenate([mixed, query_grad], axis=0).astype(jnp.bfloat16)
        by_key = jnp.concatenate([key_grad, value_grad], axis=1).astype(jnp.bfloat16)
        for context in range(contexts):
            span = slice(context * rows, (context + 1) * rows)
            results = (
                matmul_nt(scatter_ref[context], by_query[:, span]),
                matmul(scatter_ref[context], by_key[span, :]),
            )
            for t in range(4):
                j = t * heads + head
                back_ref[context, :, j * HDIM : (j + 1) * HDIM] = results[t // 2][
                    :, t % 2 * HDIM : (t % 2 + 1) * HDIM
                ].astype(jnp.bfloat16)

    departures = []
    for context in range(contexts):
        for rank in range(SLOTS):
            chunks = []
            for first in range(rank * groups, (rank + 1) * groups, pieces):
                chunks.append(
                    jnp.concatenate(
                        [
                            back_ref[context, first : first + pieces, j * HDIM : (j + 1) * HDIM]
                            for j in range(pieces)
                        ],
                        axis=0,
                    )
                )
            swapped = matmul(swap, jnp.concatenate(chunks, axis=1)).astype(jnp.bfloat16)
            for at in range(groups // pieces):
                gone_ref[
                    context, at * pieces : (at + 1) * pieces, rank * pieces : (rank + 1) * pieces, :
                ] = swapped[:, at * HDIM : (at + 1) * HDIM].reshape(pieces, pieces, HDIM)
        departures.append(
            pltpu.make_async_copy(
                gone_ref.at[context], out_ref.at[:, context], out_sem.at[context]
            )
        )
        departures[-1].start()
    for departure in departures:
        departure.wait()


def call_pack(groups, contexts, projected, out_grad, dest):
    lanes = 4 * out_grad.shape[1] // contexts
    pieces = lanes // HDIM
    whole = pl.BlockSpec(memory_space=pltpu.VMEM)
    return pl.pallas_call(
        lambda *refs: pack_kernel(groups, contexts, *refs),
        out_shape=jax.ShapeDtypeStruct((groups, contexts, SLOTS * pieces, HDIM), jnp.bfloat16),
        in_specs=[whole] * 3,
        out_specs=pl.BlockSpec(memory_space=pl.ANY),
        scratch_shapes=[
            pltpu.VMEM((2, SLOTS * groups * pieces, HDIM), jnp.float32),
            pltpu.VMEM((contexts, groups, SLOTS * pieces, HDIM), jnp.bfloat16),
            pltpu.SemaphoreType.DMA((contexts,)),
        ],
        compiler_params=pltpu.CompilerParams(vmem_limit_bytes=56 * MIB),
        name="pack",
    )(projected, out_grad, dest)


def call_plan(groups, contexts, planes, dest):
    whole = pl.BlockSpec(memory_space=pltpu.VMEM)
    return pl.pallas_call(
        lambda *refs: plan_kernel(groups, contexts, *refs),
        out_shape=jax.ShapeDtypeStruct((planes, 1, HDIM), jnp.int32),
        in_specs=[whole],
        out_specs=whole,
        compiler_params=pltpu.CompilerParams(vmem_limit_bytes=8 * MIB),
        name="plan",
    )(dest)


def call_prepare(rows, places, lengths):
    contexts, groups, _ = places.shape
    whole = pl.BlockSpec(memory_space=pltpu.VMEM)
    return pl.pallas_call(
        lambda *refs: prepare_kernel(rows, *refs),
        out_shape=(
            jax.ShapeDtypeStruct((contexts, SLOTS * groups, rows), jnp.bfloat16),
            jax.ShapeDtypeStruct((contexts * rows, contexts * rows), jnp.float32),
        ),
        in_specs=[whole, pl.BlockSpec(memory_space=pltpu.SMEM)],
        out_specs=(whole, whole),
        compiler_params=pltpu.CompilerParams(vmem_limit_bytes=12 * MIB),
        name="prepare",
    )(places, lengths)


def call_attend(contexts, rows, arrived, places, scatters, bias):
    devices, lines, _ = arrived.shape
    groups = devices // contexts
    lanes = lines // SLOTS * HDIM
    whole = pl.BlockSpec(memory_space=pltpu.VMEM)
    far = pl.BlockSpec(memory_space=pl.ANY)
    blocks = pltpu.VMEM((contexts, groups, lines, HDIM), jnp.bfloat16)
    slots = pltpu.VMEM((contexts, SLOTS * groups, lanes), jnp.bfloat16)
    return pl.pallas_call(
        attend_kernel,
        out_shape=jax.ShapeDtypeStruct((groups, contexts, lines, HDIM), jnp.bfloat16),
        in_specs=[whole, whole, far, far],
        out_specs=far,
        scratch_shapes=[
            slots,
            pltpu.VMEM((contexts * rows, lanes), jnp.bfloat16),
            slots,
            blocks,
            pltpu.VMEM((contexts * rows, contexts * rows), jnp.float32),
            pltpu.VMEM((contexts, SLOTS * groups, rows), jnp.bfloat16),
            pltpu.SemaphoreType.DMA((2,)),
            pltpu.SemaphoreType.DMA((contexts,)),
        ],
        compiler_params=pltpu.CompilerParams(vmem_limit_bytes=36 * MIB),
        name="attend",
    )(arrived.reshape(groups, contexts, lines, HDIM), places, scatters, bias)


def call_unpack(groups, contexts, returned, dest):
    rows = dest.shape[1]
    lines = returned.shape[2]
    part = lines // (SLOTS * 4) * HDIM
    width = contexts * part
    whole = pl.BlockSpec(memory_space=pltpu.VMEM)
    far = pl.BlockSpec(memory_space=pl.ANY)
    return pl.pallas_call(
        lambda *refs: unpack_kernel(groups, contexts, *refs),
        out_shape=(
            jax.ShapeDtypeStruct((rows, width), jnp.bfloat16),
            jax.ShapeDtypeStruct((rows, 3 * width), jnp.bfloat16),
        ),
        in_specs=[whole, whole],
        out_specs=(far, far),
        scratch_shapes=[
            pltpu.VMEM((contexts, 4, rows, part), jnp.bfloat16),
            pltpu.SemaphoreType.DMA((contexts, 4)),
        ],
        compiler_params=pltpu.CompilerParams(vmem_limit_bytes=20 * MIB),
        name="unpack",
    )(returned, dest)


def on_device(projected, out_grad, dest_row, lengths):
    rows = out_grad.shape[0]
    planes, contexts = lax.axis_size("z"), lax.axis_size("ctx")
    groups = lax.axis_size(DP)
    everyone = DP + ("ctx",)
    dest = dest_row.reshape(1, rows)

    plan = call_plan(groups, contexts, planes, dest)
    plan = lax.all_to_all(plan, "z", 0, 0, tiled=True).reshape(planes, HDIM)
    sent = call_pack(groups, contexts, projected, out_grad, dest)
    lines = sent.shape[2]
    arrived = lax.all_to_all(sent.reshape(-1, lines, HDIM), everyone, 0, 0, tiled=True)
    places = plan
    for axis in ("ctx", "core", "x"):
        places = lax.all_gather(places, axis, axis=0)
    places = jnp.transpose(places, (2, 3, 0, 1, 4)).reshape(contexts, groups, HDIM)
    scatters, bias = call_prepare(rows, places, lengths)
    answers = call_attend(contexts, rows, arrived, places, scatters, bias)
    returned = lax.all_to_all(
        answers.reshape(-1, lines, HDIM), everyone, 0, 0, tiled=True
    )
    return call_unpack(
        groups, contexts, returned.reshape(groups, contexts, lines, HDIM), dest
    )


def solution(mesh):
    parts = Mesh(mesh.devices.reshape(8, 4, 2, -1), DP + ("ctx",))
    everyone = DP + ("ctx",)
    return jax.shard_map(
        on_device,
        mesh=parts,
        in_specs=(P(everyone, None), P(everyone, None), P(everyone), P(DP, None)),
        out_specs=(P(everyone, None), P(everyone, None)),
        check_vma=False,
    )
```

```python
import math

import jax
import jax.numpy as jnp
from jax import lax
from jax.experimental import pallas as pl
from jax.experimental.pallas import tpu as pltpu
from jax.sharding import Mesh, PartitionSpec as P

DP = ("z", "x", "core")
HDIM = 128
SLOTS = 3
LOWEST = -1e30
MIB = 1024 * 1024


def swap_matrix(side):
    rows = lax.broadcasted_iota(jnp.int32, (side * side, side * side), 0)
    cols = lax.broadcasted_iota(jnp.int32, (side * side, side * side), 1)
    partner = (rows % side) * side + rows // side
    return (cols == partner).astype(jnp.bfloat16)


def iota(shape, axis):
    return lax.broadcasted_iota(jnp.int32, shape, axis)


def matmul(left, right):
    return jnp.dot(left, right, preferred_element_type=jnp.float32)


def matmul_nt(left, right):
    return lax.dot_general(
        left, right, (((1,), (1,)), ((), ())), preferred_element_type=jnp.float32
    )


def slot_of_rows(dest, groups, contexts, rows):
    target = dest // (rows * contexts)
    across = jnp.broadcast_to(target.astype(jnp.float32), (rows, rows))
    down = jnp.transpose(across)
    earlier = lax.broadcasted_iota(jnp.int32, (rows, rows), 0) < lax.broadcasted_iota(
        jnp.int32, (rows, rows), 1
    )
    same = jnp.where(jnp.logical_and(across == down, earlier), 1.0, 0.0)
    rank = jnp.sum(same, axis=0, keepdims=True).astype(jnp.int32)
    return rank * groups + target


def plan_kernel(groups, contexts, dest_ref, out_ref):
    rows = dest_ref.shape[1]
    planes = out_ref.shape[0]
    spots = groups // planes
    dest = dest_ref[...]
    slot = slot_of_rows(dest, groups, contexts, rows)
    group, rank = slot % groups, slot // groups
    local = (dest % rows + 1).astype(jnp.float32)
    held = jnp.where(iota((planes, rows), 0) == group // spots, local, 0.0)
    lanes = (iota((HDIM, rows), 0) == rank * spots + group % spots).astype(jnp.bfloat16)
    table = matmul_nt(held.astype(jnp.bfloat16), lanes).astype(jnp.int32)
    base = lax.axis_index("ctx") * rows
    out_ref[...] = jnp.where(table > 0, table + base, 0).reshape(out_ref.shape)


def pack_kernel(groups, contexts, proj_ref, cot_ref, dest_ref, out_ref, gone_ref, sem):
    rows = proj_ref.shape[0]
    width = cot_ref.shape[1]
    part = width // contexts
    pieces = 4 * part // HDIM
    slot = slot_of_rows(dest_ref[...], groups, contexts, rows)
    slots = SLOTS * groups
    pick = (iota((slots, rows), 0) == slot).astype(jnp.bfloat16)
    swap = swap_matrix(pieces)
    departures = []
    for share in range(contexts):
        begin = share * part
        picked = []
        for t in range(4):
            source, at = (proj_ref, t * width + begin) if t < 3 else (cot_ref, begin)
            picked.append(matmul(pick, source[:, at : at + part]).astype(jnp.bfloat16))
        picked = jnp.concatenate(picked, axis=1)
        for rank in range(SLOTS):
            chunks = []
            for first in range(rank * groups, (rank + 1) * groups, pieces):
                chunks.append(
                    jnp.concatenate(
                        [
                            picked[first : first + pieces, j * HDIM : (j + 1) * HDIM]
                            for j in range(pieces)
                        ],
                        axis=0,
                    )
                )
            swapped = matmul(swap, jnp.concatenate(chunks, axis=1)).astype(jnp.bfloat16)
            for at in range(groups // pieces):
                gone_ref[
                    share, at * pieces : (at + 1) * pieces, rank * pieces : (rank + 1) * pieces, :
                ] = swapped[:, at * HDIM : (at + 1) * HDIM].reshape(pieces, pieces, HDIM)
        departures.append(
            pltpu.make_async_copy(gone_ref.at[share], out_ref.at[:, share], sem.at[share])
        )
        departures[-1].start()
    for departure in departures:
        departure.wait()


def unpack_kernel(
    groups,
    contexts,
    in_ref,
    dest_ref,
    attended_ref,
    grad_ref,
    gone_ref,
    out_sem,
):
    rows, width = attended_ref.shape
    part = width // contexts
    pieces = 4 * part // HDIM
    slot = slot_of_rows(dest_ref[...], groups, contexts, rows)
    slots = SLOTS * groups
    slot_down = jnp.transpose(jnp.broadcast_to(slot.astype(jnp.float32), (rows, rows)))[:, :1]
    pick = (iota((rows, slots), 1) == slot_down.astype(jnp.int32)).astype(jnp.bfloat16)
    swap = swap_matrix(pieces)
    departures = []
    for share in range(contexts):
        stacked = []
        for rank in range(SLOTS):
            chunks = jnp.concatenate(
                [
                    in_ref[
                        first : first + pieces, share, rank * pieces : (rank + 1) * pieces, :
                    ].reshape(pieces * pieces, HDIM)
                    for first in range(0, groups, pieces)
                ],
                axis=1,
            )
            swapped = matmul(swap, chunks).astype(jnp.bfloat16)
            for at in range(groups // pieces):
                stacked.append(
                    jnp.concatenate(
                        [
                            swapped[j * pieces : (j + 1) * pieces, at * HDIM : (at + 1) * HDIM]
                            for j in range(pieces)
                        ],
                        axis=1,
                    )
                )
        result = matmul(pick, jnp.concatenate(stacked, axis=0)).astype(jnp.bfloat16)
        begin = share * part
        for t in range(4):
            gone_ref[share, t] = result[:, t * part : (t + 1) * part]
            target, at = (grad_ref, (t - 1) * width + begin) if t else (attended_ref, begin)
            target = target.at[:, pl.ds(at, part)]
            departures.append(
                pltpu.make_async_copy(gone_ref.at[share, t], target, out_sem.at[share, t])
            )
            departures[-1].start()
    for departure in departures:
        departure.wait()


def attend_kernel(
    in_ref,
    place_ref,
    lengths_ref,
    out_ref,
    slot_ref,
    row_ref,
    back_ref,
    gone_ref,
    out_sem,
):
    groups, contexts, lines, _ = in_ref.shape
    pieces = lines // SLOTS
    heads = pieces // 4
    rows = row_ref.shape[0] // contexts
    spots = lax.axis_size("x") * lax.axis_size("core")
    swap = swap_matrix(pieces)

    scatters, gathers = [], []
    for context in range(contexts):
        downs, acrosses = [], []
        for rank in range(SLOTS):
            lane = rank * spots + lax.axis_index("x") * lax.axis_size("core")
            lane = lane + lax.axis_index("core")
            place = place_ref[context].astype(jnp.float32)
            place = jnp.where(iota((groups, HDIM), 1) == lane, place, 0.0)
            down = jnp.sum(place, axis=1, keepdims=True) - (context * rows + 1.0)
            downs.append(down.astype(jnp.int32))
            spread = jnp.broadcast_to(down, (groups, HDIM))
            acrosses.append(jnp.transpose(spread)[:1, :])
        place_down = jnp.concatenate(downs, axis=0)
        place_across = jnp.concatenate(acrosses, axis=1).astype(jnp.int32)
        slots = SLOTS * groups
        gathers.append((iota((rows, slots), 0) == place_across).astype(jnp.bfloat16))
        scatters.append((iota((slots, rows), 1) == place_down).astype(jnp.bfloat16))

    end0 = lengths_ref[0, 0]
    end1 = end0 + lengths_ref[0, 1]
    end2 = end1 + lengths_ref[0, 2]

    def segment(axis):
        position = iota((contexts * rows, contexts * rows), axis)
        return (
            (position >= end0).astype(jnp.int32)
            + (position >= end1).astype(jnp.int32)
            + (position >= end2).astype(jnp.int32)
        )

    bias = jnp.where(segment(0) == segment(1), 0.0, LOWEST)

    for context in range(contexts):
        for rank in range(SLOTS):
            chunks = jnp.concatenate(
                [
                    in_ref[
                        first : first + pieces, context, rank * pieces : (rank + 1) * pieces, :
                    ].reshape(pieces * pieces, HDIM)
                    for first in range(0, groups, pieces)
                ],
                axis=1,
            )
            swapped = matmul(swap, chunks).astype(jnp.bfloat16)
            for at in range(groups // pieces):
                begin = rank * groups + at * pieces
                for j in range(pieces):
                    slot_ref[context, begin : begin + pieces, j * HDIM : (j + 1) * HDIM] = swapped[
                        j * pieces : (j + 1) * pieces, at * HDIM : (at + 1) * HDIM
                    ]
        row_ref[context * rows : (context + 1) * rows, :] = matmul(
            gathers[context], slot_ref[context]
        ).astype(jnp.bfloat16)

    scale = 1.0 / math.sqrt(HDIM)
    for head in range(heads):
        query, key, value, cotangent = [
            row_ref[:, (t * heads + head) * HDIM : (t * heads + head + 1) * HDIM]
            for t in range(4)
        ]
        scores = matmul_nt(key, query) * (scale * math.log2(math.e)) + bias
        top = jnp.max(scores, axis=0, keepdims=True)
        powers = jnp.exp2(scores - top)
        total = jnp.sum(powers, axis=0, keepdims=True)
        exact = powers * (1.0 / total)
        weights = exact.astype(jnp.bfloat16)
        mixed = matmul(jnp.transpose(value), weights)
        drift = jnp.sum(
            jnp.transpose(cotangent).astype(jnp.float32) * mixed, axis=0, keepdims=True
        )
        pulls = matmul_nt(value, cotangent)
        slopes = (exact * ((pulls - drift) * scale)).astype(jnp.bfloat16)
        query_grad = matmul(jnp.transpose(key), slopes)
        key_grad = matmul(slopes, query)
        value_grad = matmul(weights, cotangent)
        by_query = jnp.concatenate([mixed, query_grad], axis=0).astype(jnp.bfloat16)
        by_key = jnp.concatenate([key_grad, value_grad], axis=1).astype(jnp.bfloat16)
        for context in range(contexts):
            span = slice(context * rows, (context + 1) * rows)
            results = (
                matmul_nt(scatters[context], by_query[:, span]),
                matmul(scatters[context], by_key[span, :]),
            )
            for t in range(4):
                j = t * heads + head
                back_ref[context, :, j * HDIM : (j + 1) * HDIM] = results[t // 2][
                    :, t % 2 * HDIM : (t % 2 + 1) * HDIM
                ].astype(jnp.bfloat16)

    departures = []
    for context in range(contexts):
        for rank in range(SLOTS):
            chunks = []
            for first in range(rank * groups, (rank + 1) * groups, pieces):
                chunks.append(
                    jnp.concatenate(
                        [
                            back_ref[context, first : first + pieces, j * HDIM : (j + 1) * HDIM]
                            for j in range(pieces)
                        ],
                        axis=0,
                    )
                )
            swapped = matmul(swap, jnp.concatenate(chunks, axis=1)).astype(jnp.bfloat16)
            for at in range(groups // pieces):
                gone_ref[
                    context, at * pieces : (at + 1) * pieces, rank * pieces : (rank + 1) * pieces, :
                ] = swapped[:, at * HDIM : (at + 1) * HDIM].reshape(pieces, pieces, HDIM)
        departures.append(
            pltpu.make_async_copy(
                gone_ref.at[context], out_ref.at[:, context], out_sem.at[context]
            )
        )
        departures[-1].start()
    for departure in departures:
        departure.wait()


def call_pack(groups, contexts, projected, out_grad, dest):
    lanes = 4 * out_grad.shape[1] // contexts
    pieces = lanes // HDIM
    whole = pl.BlockSpec(memory_space=pltpu.VMEM)
    return pl.pallas_call(
        lambda *refs: pack_kernel(groups, contexts, *refs),
        out_shape=jax.ShapeDtypeStruct((groups, contexts, SLOTS * pieces, HDIM), jnp.bfloat16),
        in_specs=[whole] * 3,
        out_specs=pl.BlockSpec(memory_space=pl.ANY),
        scratch_shapes=[
            pltpu.VMEM((contexts, groups, SLOTS * pieces, HDIM), jnp.bfloat16),
            pltpu.SemaphoreType.DMA((contexts,)),
        ],
        compiler_params=pltpu.CompilerParams(vmem_limit_bytes=56 * MIB),
        name="pack",
    )(projected, out_grad, dest)


def call_plan(groups, contexts, planes, dest):
    whole = pl.BlockSpec(memory_space=pltpu.VMEM)
    return pl.pallas_call(
        lambda *refs: plan_kernel(groups, contexts, *refs),
        out_shape=jax.ShapeDtypeStruct((planes, 1, HDIM), jnp.int32),
        in_specs=[whole],
        out_specs=whole,
        compiler_params=pltpu.CompilerParams(vmem_limit_bytes=8 * MIB),
        name="plan",
    )(dest)


def call_attend(contexts, rows, arrived, places, lengths):
    devices, lines, _ = arrived.shape
    groups = devices // contexts
    lanes = lines // SLOTS * HDIM
    whole = pl.BlockSpec(memory_space=pltpu.VMEM)
    far = pl.BlockSpec(memory_space=pl.ANY)
    blocks = pltpu.VMEM((contexts, groups, lines, HDIM), jnp.bfloat16)
    slots = pltpu.VMEM((contexts, SLOTS * groups, lanes), jnp.bfloat16)
    return pl.pallas_call(
        attend_kernel,
        out_shape=jax.ShapeDtypeStruct((groups, contexts, lines, HDIM), jnp.bfloat16),
        in_specs=[whole, whole, pl.BlockSpec(memory_space=pltpu.SMEM)],
        out_specs=far,
        scratch_shapes=[
            slots,
            pltpu.VMEM((contexts * rows, lanes), jnp.bfloat16),
            slots,
            blocks,
            pltpu.SemaphoreType.DMA((contexts,)),
        ],
        compiler_params=pltpu.CompilerParams(vmem_limit_bytes=36 * MIB),
        name="attend",
    )(arrived.reshape(groups, contexts, lines, HDIM), places, lengths)


def call_unpack(groups, contexts, returned, dest):
    rows = dest.shape[1]
    lines = returned.shape[2]
    part = lines // (SLOTS * 4) * HDIM
    width = contexts * part
    whole = pl.BlockSpec(memory_space=pltpu.VMEM)
    far = pl.BlockSpec(memory_space=pl.ANY)
    return pl.pallas_call(
        lambda *refs: unpack_kernel(groups, contexts, *refs),
        out_shape=(
            jax.ShapeDtypeStruct((rows, width), jnp.bfloat16),
            jax.ShapeDtypeStruct((rows, 3 * width), jnp.bfloat16),
        ),
        in_specs=[whole, whole],
        out_specs=(far, far),
        scratch_shapes=[
            pltpu.VMEM((contexts, 4, rows, part), jnp.bfloat16),
            pltpu.SemaphoreType.DMA((contexts, 4)),
        ],
        compiler_params=pltpu.CompilerParams(vmem_limit_bytes=20 * MIB),
        name="unpack",
    )(returned, dest)


def on_device(projected, out_grad, dest_row, lengths):
    rows = out_grad.shape[0]
    planes, contexts = lax.axis_size("z"), lax.axis_size("ctx")
    groups = lax.axis_size(DP)
    everyone = DP + ("ctx",)
    dest = dest_row.reshape(1, rows)

    plan = call_plan(groups, contexts, planes, dest)
    plan = lax.all_to_all(plan, "z", 0, 0, tiled=True).reshape(planes, HDIM)
    sent = call_pack(groups, contexts, projected, out_grad, dest)
    lines = sent.shape[2]
    arrived = lax.all_to_all(sent.reshape(-1, lines, HDIM), everyone, 0, 0, tiled=True)
    places = plan
    for axis in ("ctx", "core", "x"):
        places = lax.all_gather(places, axis, axis=0)
    places = jnp.transpose(places, (2, 3, 0, 1, 4)).reshape(contexts, groups, HDIM)
    answers = call_attend(contexts, rows, arrived, places, lengths)
    returned = lax.all_to_all(
        answers.reshape(-1, lines, HDIM), everyone, 0, 0, tiled=True
    )
    return call_unpack(
        groups, contexts, returned.reshape(groups, contexts, lines, HDIM), dest
    )


def solution(mesh):
    parts = Mesh(mesh.devices.reshape(8, 4, 2, -1), DP + ("ctx",))
    everyone = DP + ("ctx",)
    return jax.shard_map(
        on_device,
        mesh=parts,
        in_specs=(P(everyone, None), P(everyone, None), P(everyone), P(DP, None)),
        out_specs=(P(everyone, None), P(everyone, None)),
        check_vma=False,
    )
```
